32 devices in a mesh: dp: 8 (over z, x), mp: 4 (over y, core).
Axes of the slice: x: 2, y: 2, z: 4, core: 2. Of those that a mesh axis runs over, the one named last changes fastest.
Arguments:
- layer_input: bfloat16 [12288, 1024], P(('dp', 'mp')), may hold values from -6 to 6
- row_seq: int32 [12288], P(('dp', 'mp')), may hold values from -1 to 11, as said below
- qkv_weight: bfloat16 [1024, 3, 1024], P('dp', None, 'mp'), may hold values from -0.25 to 0.25
- out_weight: bfloat16 [1024, 1024], P('mp', 'dp'), may hold values from -0.75 to 0.75
- in_weight: bfloat16 [1024, 2, 2624], P('dp', None, 'mp'), may hold values from -0.1875 to 0.1875
- down_weight: bfloat16 [2624, 1024], P('mp', 'dp'), may hold values from -0.125 to 0.125
- attn_gain: bfloat16 [1024], P('dp'), may hold values from 0.099609375 to 1.8984375
- mlp_gain: bfloat16 [1024], P('dp'), may hold values from 0.099609375 to 1.8984375
- cotangent: bfloat16 [12288, 1024], P(('dp', 'mp')), may hold values from -6 to 6
Outputs:
- activations: bfloat16 [12288, 1024], P(('dp', 'mp'))
- input_grad: bfloat16 [12288, 1024], P(('dp', 'mp'))
- attn_gain_grad: float32 [1024], P('dp')
- mlp_gain_grad: float32 [1024], P('dp')
- qkv_grad: float32 [1024, 3, 1024], P('dp', None, 'mp')
- out_grad: float32 [1024, 1024], P('mp', 'dp')
- in_grad: float32 [1024, 2, 2624], P('dp', None, 'mp')
- down_grad: float32 [2624, 1024], P('mp', 'dp')
The draws below stay inside these ranges and needn't reach their ends.
Inputs may be any that keep to these rules, and one draw needn't show every extreme that they name: `row_seq`: rows come in groups of 1536 (one index of dp, 12 blocks of 128 rows). In each group the sequence numbers rise from 0 without gaps, each sequence's rows are contiguous and start at a multiple of 128, a sequence has at most 1024 rows, padding (-1) stands only at the end of a sequence's last block and in whole blocks after a group's last sequence. Some group has sequences in all its blocks and begins with one of exactly 1024 rows; another group has a sequence starting in each of its blocks.
All inputs are finite; a program needn't handle non-finite values.
Results may differ from the reference program's by a relative error of at most 0.022.
Values may be sent and summed in bfloat16 or wider, within the bound.
A program may use at most 128 MiB of HBM per device.

```python
import math
import jax
import jax.numpy as jnp
from jax import lax

D = 1024
HEADS = 16
HEAD_DIM = 64
FF = 2624
WIN = 128
QUERY_ROWS = 512
CAP = 12
GROUP_ROWS = 1536
SEQ_MAX = 1024
ROWS = 12288
N_DP = 8


def draw_row_seq(key, part):
    key = jax.random.fold_in(key, 11)
    fill_key, pick_key, coin_key, tail_key = jax.random.split(key, 4)
    group_count = N_DP
    block_count = CAP
    longest = SEQ_MAX // WIN
    group_index = jnp.arange(group_count, dtype=jnp.int32)
    chosen = jax.random.randint(pick_key, (), 0, group_count, dtype=jnp.int32)
    special = group_index == chosen
    dense = group_index == (chosen + 1) % group_count
    filled = jax.random.randint(fill_key, (group_count,), block_count // 4, block_count + 1, dtype=jnp.int32)
    filled = jnp.maximum(jnp.where(special | dense, block_count, filled), 1)
    coins = jax.random.randint(coin_key, (block_count, group_count), 0, 3, dtype=jnp.int32) == 0
    tails = jax.random.randint(tail_key, (block_count, group_count), 1, WIN + 1, dtype=jnp.int32)
    block_index = jnp.arange(block_count, dtype=jnp.int32)

    def advance(run_length, inputs):
        position, coin = inputs
        opens = (position == 0) | coin | (run_length >= longest)
        forced = jnp.where(position < longest, position == 0, jnp.where(position == longest, True, opens))
        opens = jnp.where(special, forced, opens)
        opens = jnp.where(dense, True, opens)
        run_length = jnp.where(opens, 1, run_length + 1)
        return (run_length, opens)
    _, starts = lax.scan(advance, jnp.zeros((group_count,), jnp.int32), (block_index, coins))
    following = jnp.concatenate([starts[1:], jnp.ones((1, group_count), jnp.bool_)], axis=0)
    closing = following | (block_index[:, None] + 1 >= filled[None, :])
    tails = jnp.where(special[None, :] & (block_index[:, None] == longest - 1), WIN, tails)
    live_count = jnp.where(block_index[:, None] >= filled[None, :], 0, jnp.where(closing, tails, WIN))
    numbers = jnp.cumsum(starts.astype(jnp.int32), axis=0) - 1
    token_index = jnp.arange(WIN, dtype=jnp.int32)
    table = jnp.where(token_index[None, None, :] < live_count[:, :, None], numbers[:, :, None], -1)
    return jnp.transpose(table, (1, 0, 2)).reshape(group_count * block_count * WIN).astype(jnp.int32)


def with_spikes(drawn, key, source, target, blocks, factor):
    owner, partner = [(jnp.arange(drawn.shape[dim]) // (drawn.shape[dim] // blocks)).reshape([-1 if axis == dim else 1 for axis in range(drawn.ndim)]) for dim in (source, target)]
    chosen = jax.random.permutation(key, blocks)[partner]
    strong = (owner == chosen) | (owner == (partner + blocks // 2) % blocks)
    return jnp.where(strong, factor * drawn, drawn)


def block_scale(stream_key, extent, cuts, least, top_value):
    loudness, own = 1.0, jax.random.fold_in(stream_key, 6)
    for dim, parts in cuts:
        draws = jnp.exp(jax.random.uniform(jax.random.fold_in(own, dim), (parts,), jnp.float32, least / len(cuts), top_value / len(cuts)))
        loudness = loudness * jnp.repeat(draws, extent[dim] // parts).reshape([-1 if axis == dim else 1 for axis in range(len(extent))])
    return loudness


def bell_draw(rng, dims, scale, bound, cuts=(), kind=jnp.bfloat16):
    values = scale * jax.random.normal(rng, dims, jnp.float32)
    if cuts:
        values = values * block_scale(rng, dims, cuts, -0.22, 0.18)
    return jnp.clip(values, -bound, bound).astype(kind)


def gaussian_with(rng, dims, scale, limit, shards, heavy, kind=jnp.bfloat16):
    drawn = scale * jax.random.normal(rng, dims, jnp.float32)
    if shards:
        drawn = drawn * block_scale(rng, dims, shards, -0.22, 0.18)
    return jnp.clip(with_spikes(drawn, jax.random.fold_in(rng, 3), *heavy), -limit, limit).astype(kind)


def setup_inputs(seed: int = 0) -> dict:
    key_list = jax.random.split(jax.random.key(seed), 10)
    return {
        "layer_input": bell_draw(key_list[0], (ROWS, D), 1.0, 6.0, ((0, 32),)),
        "row_seq": draw_row_seq(jax.random.fold_in(key_list[9], 71), 0),
        "qkv_weight": bell_draw(key_list[2], (D, 3, D), (D // 2) ** -0.5, 0.25, ((0, 8), (2, 4))),
        "out_weight": bell_draw(key_list[3], (D, D), (D // 16) ** -0.5, 0.75, ((0, 4), (1, 8))),
        "in_weight": bell_draw(key_list[4], (D, 2, FF), D ** -0.5, 0.1875, ((0, 8), (2, 4))),
        "down_weight": bell_draw(key_list[5], (FF, D), FF ** -0.5, 0.125, ((0, 4), (1, 8))),
        "attn_gain": jnp.clip(1.0 + 0.18 * jax.random.normal(key_list[6], (D,), jnp.float32), 0.099609375, 1.8984375).astype(jnp.bfloat16),
        "mlp_gain": jnp.clip(1.0 + 0.18 * jax.random.normal(key_list[7], (D,), jnp.float32), 0.099609375, 1.8984375).astype(jnp.bfloat16),
        "cotangent": gaussian_with(key_list[8], (ROWS, D), 1.0, 6.0, ((0, 32),), (0, 1, 32, 2.75)),
    }


@jax.custom_vjp
def low(v):
    return lax.optimization_barrier(v.astype(jnp.bfloat16)).astype(jnp.float32)

@jax.custom_vjp
def low_back(v):
    return v

def low_keep(v):
    return (low(v), None)

def low_pass(kept, grad):
    return (grad,)

def back_keep(v):
    return (v, None)

def back_low(kept, grad):
    return (low(grad),)
low.defvjp(low_keep, low_pass)
low_back.defvjp(back_keep, back_low)
EPSILON = 1e-05
THETA_BASE = 10000.0
HIGHEST = lax.Precision.HIGHEST

def normalize(block_in):
    row_mean = lax.optimization_barrier(jnp.mean(block_in, axis=-1, keepdims=True))
    centred = block_in - row_mean
    variance = lax.optimization_barrier(jnp.mean(centred * centred, axis=-1, keepdims=True))
    return centred * lax.rsqrt(variance + EPSILON)

def positions(sequence):
    length = sequence.shape[0]
    row_index = jnp.arange(length, dtype=jnp.int32)
    before = jnp.concatenate([jnp.full((1,), -7, jnp.int32), sequence[:-1]])
    run_start = lax.cummax(jnp.where(sequence != before, row_index, 0), axis=0)
    return row_index - run_start

def rotation(place, width):
    half_width = width // 2
    frequency = jnp.exp(jnp.arange(half_width, dtype=jnp.float32) * (-2.0 * math.log(THETA_BASE) / width))
    angles = place.astype(jnp.float32)[:, None] * frequency[None, :]
    return (jnp.cos(angles), jnp.sin(angles))

def rotate(tensor, cosine, sine_table):
    half_width = tensor.shape[-1] // 2
    first_half = tensor[..., :half_width]
    second_half = tensor[..., half_width:]
    cos_rows = cosine[:, None, :]
    sin_rows = sine_table[:, None, :]
    return jnp.concatenate([first_half * cos_rows - second_half * sin_rows, second_half * cos_rows + first_half * sin_rows], axis=-1)

def allowed_pairs(sequence, padded_sequence, offset, half_window, key_span):
    query_seq = lax.dynamic_slice_in_dim(sequence, offset, QUERY_ROWS, 0)
    key_seq = lax.dynamic_slice_in_dim(padded_sequence, offset, key_span, 0)
    query_place = offset + jnp.arange(QUERY_ROWS, dtype=jnp.int32)
    key_place = offset - half_window + jnp.arange(key_span, dtype=jnp.int32)
    distance = jnp.abs(query_place[:, None] - key_place[None, :])
    same_run = (query_seq[:, None] == key_seq[None, :]) & (query_seq[:, None] >= 0) & (distance <= half_window)
    return same_run | (distance == 0)

def attend(queries, key_rows, value_rows, sequence):
    group_rows, width = queries.shape
    half_window = WIN // 2
    key_span = QUERY_ROWS + 2 * half_window
    padded_keys = jnp.pad(key_rows, ((half_window, half_window), (0, 0)))
    padded_values = jnp.pad(value_rows, ((half_window, half_window), (0, 0)))
    padded_sequence = jnp.pad(sequence, (half_window, half_window), constant_values=-5)
    factor = 1.0 / math.sqrt(HEAD_DIM)

    def one_block(offset):
        q_block = lax.dynamic_slice_in_dim(queries, offset, QUERY_ROWS, 0).reshape(QUERY_ROWS, HEADS, HEAD_DIM)
        k_block = lax.dynamic_slice_in_dim(padded_keys, offset, key_span, 0).reshape(key_span, HEADS, HEAD_DIM)
        v_block = lax.dynamic_slice_in_dim(padded_values, offset, key_span, 0).reshape(key_span, HEADS, HEAD_DIM)
        allowed = allowed_pairs(sequence, padded_sequence, offset, half_window, key_span)
        scores = low_back(jnp.einsum('qhd,khd->hqk', q_block, k_block, precision=HIGHEST) * factor)
        scores = jnp.where(allowed[None], scores, -1e+30)
        row_peak = lax.optimization_barrier(jnp.max(scores, axis=-1, keepdims=True))
        weights = jnp.exp(scores - row_peak)
        probabilities = weights / lax.optimization_barrier(jnp.sum(weights, axis=-1, keepdims=True))
        block_out = jnp.einsum('hqk,khd->qhd', low(probabilities), v_block, precision=HIGHEST)
        return block_out.reshape(QUERY_ROWS, width)
    offsets = jnp.arange(group_rows // QUERY_ROWS, dtype=jnp.int32) * QUERY_ROWS
    outputs = lax.map(jax.checkpoint(one_block), offsets)
    return outputs.reshape(group_rows, width)

def split_heads(tensor):
    return tensor.reshape(tensor.shape[0], HEADS, HEAD_DIM)

def forward(block_in, sequence, w_qkv, w_out, w_in, w_down, gain_one, gain_two):
    group_rows = block_in.shape[0]
    h_one = low(normalize(block_in) * gain_one)
    qkv = low_back(jnp.einsum('rd,dcf->rcf', h_one, w_qkv, precision=HIGHEST))
    cosine, sine_table = rotation(positions(sequence), HEAD_DIM)
    queries = low(rotate(split_heads(qkv[:, 0]), cosine, sine_table).reshape(group_rows, D))
    key_rows = low(rotate(split_heads(qkv[:, 1]), cosine, sine_table).reshape(group_rows, D))
    value_rows = low(qkv[:, 2])
    mixed_heads = low(low_back(attend(queries, key_rows, value_rows, sequence)))
    middle = block_in + low_back(jnp.dot(mixed_heads, w_out, precision=HIGHEST))
    h_two = low(normalize(middle) * gain_two)
    gate_up = low_back(jnp.einsum('rd,dcf->rcf', h_two, w_in, precision=HIGHEST))
    hidden = low(jax.nn.gelu(gate_up[:, 0], approximate=False) * gate_up[:, 1])
    return middle + low_back(jnp.dot(hidden, w_down, precision=HIGHEST))

def reference(layer_input, row_seq, qkv_weight, out_weight, in_weight, down_weight, attn_gain, mlp_gain, cotangent):
    params = tuple((item.astype(jnp.float32) for item in (qkv_weight, out_weight, in_weight, down_weight, attn_gain, mlp_gain)))
    groups_in = layer_input.astype(jnp.float32).reshape(N_DP, GROUP_ROWS, D)
    groups_seq = row_seq.reshape(N_DP, GROUP_ROWS)
    groups_cot = cotangent.astype(jnp.float32).reshape(N_DP, GROUP_ROWS, D)

    def one_group(totals, inputs):
        group_in, group_seq, group_cot = inputs
        live_rows = (group_seq >= 0).astype(jnp.float32)[:, None]

        def whole_layer(block_in, w_qkv, w_out, w_in, w_down, gain_one, gain_two):
            return forward(block_in, group_seq, w_qkv, w_out, w_in, w_down, gain_one, gain_two)
        result, pullback = jax.vjp(whole_layer, group_in, *params)
        gradients = pullback(group_cot * live_rows)
        totals = tuple((total_item + grad_item for total_item, grad_item in zip(totals, gradients[1:])))
        return (totals, (result.astype(jnp.bfloat16), gradients[0].astype(jnp.bfloat16)))
    zero_sums = tuple((jnp.zeros_like(item) for item in params))
    totals, (outputs, input_grads) = lax.scan(one_group, zero_sums, (groups_in, groups_seq, groups_cot))
    return (outputs.reshape(ROWS, D), input_grads.reshape(ROWS, D), totals[4], totals[5], totals[0], totals[1], totals[2], totals[3])
```

```python
import math

import jax
import jax.numpy as jnp
from jax import lax
from jax.experimental import pallas as pl
from jax.experimental.pallas import tpu as pltpu
from jax.sharding import PartitionSpec as P

HEAD_DIM = 64
WIN = 128
EPSILON = 1e-05
THETA_BASE = 10000.0
BF16 = jnp.bfloat16
F32 = jnp.float32


def normalize(block_in):
    row_mean = jnp.mean(block_in, axis=-1, keepdims=True)
    centred = block_in - row_mean
    variance = jnp.mean(centred * centred, axis=-1, keepdims=True)
    factor = lax.rsqrt(variance + EPSILON)
    return (centred * factor, factor)


def norm_back(grad_in, normed, factor, gain):
    scaled = grad_in * gain
    centred_grad = (
        scaled
        - jnp.mean(scaled, axis=-1, keepdims=True)
        - normed * jnp.mean(scaled * normed, axis=-1, keepdims=True)
    )
    return (factor * centred_grad, jnp.sum(grad_in * normed, axis=0))


def positions(sequence):
    length = sequence.shape[0]
    row_index = jnp.arange(length, dtype=jnp.int32)
    before = jnp.concatenate([jnp.full((1,), -7, jnp.int32), sequence[:-1]])
    run_start = lax.cummax(jnp.where(sequence != before, row_index, 0), axis=0)
    return row_index - run_start


def rotation_tables(place):
    half = HEAD_DIM // 2
    frequency = jnp.exp(
        jnp.arange(half, dtype=F32) * (-2.0 * math.log(THETA_BASE) / HEAD_DIM)
    )
    angles = place.astype(F32)[:, None] * frequency[None, :]
    cosine, sine = (jnp.cos(angles), jnp.sin(angles))
    return (
        jnp.concatenate([cosine] * 4, axis=1),
        jnp.concatenate([-sine, sine, -sine, sine], axis=1),
    )


def turn(tensor, cosine, signed_sine):
    lane = lax.broadcasted_iota(jnp.int32, cosine.shape, 1)
    first = (lane % HEAD_DIM) < HEAD_DIM // 2
    parts = []
    for start in range(0, tensor.shape[1], 128):
        piece = tensor[:, start : start + 128]
        other = jnp.where(first, pltpu.roll(piece, 96, 1), pltpu.roll(piece, 32, 1))
        parts.append(piece * cosine + other * signed_sine)
    return jnp.concatenate(parts, axis=1)


def head_masks(heads, width):
    lane = lax.broadcasted_iota(jnp.int32, (WIN, width), 1)
    return [(lane // HEAD_DIM == head).astype(F32) for head in range(heads)]


def allowed_pairs(seq_col, seq_row):
    query = lax.broadcasted_iota(jnp.int32, (WIN, 2 * WIN), 0) + WIN // 2
    key = lax.broadcasted_iota(jnp.int32, (WIN, 2 * WIN), 1)
    distance = jnp.abs(query - key)
    same_run = (seq_col == seq_row) & (seq_col >= 0) & (distance <= WIN // 2)
    return same_run | (distance == 0)


def place_of(block, me, per_quarter):
    quarter = lax.div(block, per_quarter)
    start = pl.multiple_of(lax.rem(block, per_quarter) * WIN, WIN)
    return (jnp.bitwise_xor(quarter, me), pl.ds(start, WIN))


def probabilities_of(queries, keys, allowed, masks):
    heads = len(masks)
    stacked = jnp.concatenate([queries * mask.astype(BF16) for mask in masks], axis=0)
    scores = lax.dot_general(
        stacked, keys, (((1,), (1,)), ((), ())), preferred_element_type=F32
    ) * (1.0 / math.sqrt(HEAD_DIM))
    scores = scores.reshape(heads, WIN, 2 * WIN)
    scores = jnp.where(allowed[None], scores, -1e30)
    weights = jnp.exp(scores - jnp.max(scores, axis=-1, keepdims=True))
    total = jnp.sum(weights, axis=-1, keepdims=True)
    return (stacked, weights * (1.0 / total))


def forward_kernel(me_ref, qkv_ref, cos_ref, sin_ref, col_ref, row_ref, o_ref, q_ref, k_ref, v_ref):
    me = me_ref[0]
    rows, width = q_ref.shape
    blocks = rows // WIN
    per_quarter = qkv_ref.shape[1] // WIN
    half = WIN // 2
    for ref in (k_ref, v_ref):
        ref[0:half, :] = jnp.zeros((half, width), BF16)
        ref[rows + half : rows + 2 * half, :] = jnp.zeros((half, width), BF16)

    def turn_block(block, carry):
        quarter, inner = place_of(block, me, per_quarter)
        start = pl.multiple_of(block * WIN, WIN)
        here = pl.ds(start, WIN)
        later = pl.ds(pl.multiple_of(start + half, half), WIN)
        cosine, sine = (cos_ref[here, :], sin_ref[here, :])
        q_ref[here, :] = turn(qkv_ref[quarter, inner, 0:width], cosine, sine).astype(BF16)
        k_ref[later, :] = turn(qkv_ref[quarter, inner, width : 2 * width], cosine, sine).astype(BF16)
        v_ref[later, :] = qkv_ref[quarter, inner, 2 * width : 3 * width].astype(BF16)
        return carry

    lax.fori_loop(0, blocks, turn_block, 0)
    masks = head_masks(width // HEAD_DIM, width)

    def attend_block(block, carry):
        quarter, inner = place_of(block, me, per_quarter)
        start = pl.multiple_of(block * WIN, WIN)
        span = pl.ds(start, 2 * WIN)
        allowed = allowed_pairs(col_ref[pl.ds(start, WIN), :], row_ref[block])
        _, prob = probabilities_of(q_ref[pl.ds(start, WIN), :], k_ref[span, :], allowed, masks)
        prob = prob.astype(BF16).reshape(-1, 2 * WIN)
        mixed = jnp.dot(prob, v_ref[span, :], preferred_element_type=F32)
        mixed = mixed.reshape(len(masks), WIN, width)
        o_ref[quarter, inner, :] = sum(
            mixed[head] * mask for head, mask in enumerate(masks)
        ).astype(BF16)
        return carry

    lax.fori_loop(0, blocks, attend_block, 0)


def backward_kernel(
    me_ref, q_ref, k_ref, v_ref, g_ref, cos_ref, sin_ref, col_ref, row_ref, d_ref, dk_ref, dv_ref
):
    me = me_ref[0]
    rows, width = q_ref.shape
    blocks = rows // WIN
    per_quarter = g_ref.shape[1] // WIN
    half = WIN // 2
    factor = 1.0 / math.sqrt(HEAD_DIM)
    dk_ref[...] = jnp.zeros(dk_ref.shape, F32)
    dv_ref[...] = jnp.zeros(dv_ref.shape, F32)
    masks = head_masks(width // HEAD_DIM, width)
    over_rows = (((0,), (0,)), ((), ()))

    def attend_block(block, carry):
        quarter, inner = place_of(block, me, per_quarter)
        start = pl.multiple_of(block * WIN, WIN)
        here = pl.ds(start, WIN)
        span = pl.ds(start, 2 * WIN)
        allowed = allowed_pairs(col_ref[here, :], row_ref[block])
        keys = k_ref[span, :]
        queries, prob = probabilities_of(q_ref[here, :], keys, allowed, masks)
        grads = g_ref[quarter, inner, :]
        grads = jnp.concatenate([grads * mask.astype(BF16) for mask in masks], axis=0)
        grad_prob = lax.dot_general(
            grads, v_ref[span, :], (((1,), (1,)), ((), ())), preferred_element_type=F32
        ).reshape(prob.shape)
        inner_sum = jnp.sum(prob * grad_prob, axis=-1, keepdims=True)
        grad_score = (prob * (grad_prob - inner_sum)).astype(BF16).reshape(-1, 2 * WIN)
        prob = prob.astype(BF16).reshape(-1, 2 * WIN)
        dv_ref[span, :] += lax.dot_general(prob, grads, over_rows, preferred_element_type=F32)
        dk_ref[span, :] += lax.dot_general(
            grad_score, queries, over_rows, preferred_element_type=F32
        )
        grad_query = jnp.dot(grad_score, keys, preferred_element_type=F32)
        grad_query = grad_query.reshape(len(masks), WIN, width)
        grad_query = sum(grad_query[head] * mask for head, mask in enumerate(masks)) * factor
        d_ref[quarter, inner, 0:width] = turn(
            grad_query, cos_ref[here, :], -sin_ref[here, :]
        ).astype(BF16)
        return carry

    lax.fori_loop(0, blocks, attend_block, 0)

    def finish_block(block, carry):
        quarter, inner = place_of(block, me, per_quarter)
        start = pl.multiple_of(block * WIN, WIN)
        here = pl.ds(start, WIN)
        later = pl.ds(pl.multiple_of(start + half, half), WIN)
        d_ref[quarter, inner, width : 2 * width] = turn(
            dk_ref[later, :] * factor, cos_ref[here, :], -sin_ref[here, :]
        ).astype(BF16)
        d_ref[quarter, inner, 2 * width : 3 * width] = dv_ref[later, :].astype(BF16)
        return carry

    lax.fori_loop(0, blocks, finish_block, 0)


def vmem_specs(count):
    return [pl.BlockSpec(memory_space=pltpu.SMEM)] + [pl.BlockSpec(memory_space=pltpu.VMEM)] * count


def attend_forward(me, qkv, tables, width):
    quarters, share, _ = qkv.shape
    rows = quarters * share
    padded = jax.ShapeDtypeStruct((rows + WIN, width), BF16)
    return pl.pallas_call(
        forward_kernel,
        out_shape=(
            jax.ShapeDtypeStruct((quarters, share, width), BF16),
            jax.ShapeDtypeStruct((rows, width), BF16),
            padded,
            padded,
        ),
        in_specs=vmem_specs(5),
        out_specs=(pl.BlockSpec(memory_space=pltpu.VMEM),) * 4,
        compiler_params=pltpu.CompilerParams(vmem_limit_bytes=40 * 2**20),
        cost_estimate=pl.CostEstimate(
            flops=16 * rows * WIN * width, bytes_accessed=16 * rows * width, transcendentals=0
        ),
        name="attend_forward",
    )(me, qkv, *tables)


def attend_backward(me, queries, keys, values, grads, tables):
    quarters, share, width = grads.shape
    rows = quarters * share
    accumulator = pltpu.VMEM((rows + WIN, width), F32)
    return pl.pallas_call(
        backward_kernel,
        out_shape=jax.ShapeDtypeStruct((quarters, share, 3 * width), BF16),
        in_specs=vmem_specs(8),
        out_specs=pl.BlockSpec(memory_space=pltpu.VMEM),
        scratch_shapes=[accumulator, accumulator],
        compiler_params=pltpu.CompilerParams(vmem_limit_bytes=40 * 2**20),
        cost_estimate=pl.CostEstimate(
            flops=40 * rows * WIN * width, bytes_accessed=16 * rows * width, transcendentals=0
        ),
        name="attend_backward",
    )(me, queries, keys, values, grads, *tables)


def swap(tensor, bit):
    return lax.ppermute(tensor, "mp", [(i, i ^ bit) for i in range(4)])


def spread(rows):
    across = swap(rows, 2)
    return [rows, swap(rows, 1), across, swap(across, 1)]


def collect(product):
    away = [swap(product(r).astype(BF16), 1) for r in (3, 1)]
    across = swap((product(2) + away[0].astype(F32)).astype(BF16), 2)
    return product(0) + away[1].astype(F32) + across.astype(F32)


def dot_nt(left, right):
    return lax.dot_general(left, right, (((1,), (1,)), ((), ())), preferred_element_type=F32)


def dot_tn(left, right):
    return lax.dot_general(left, right, (((0,), (0,)), ((), ())), preferred_element_type=F32)


def gather_columns(shard):
    parts = lax.all_gather(shard, "dp", axis=0)
    return jnp.transpose(parts, (1, 0, 2)).reshape(shard.shape[0], -1)


def scatter_rows(grad):
    return lax.psum_scatter(grad.astype(BF16), "dp", scatter_dimension=0, tiled=True).astype(F32)


def scatter_columns(grad):
    n = lax.axis_size("dp")
    parts = jnp.transpose(grad.astype(BF16).reshape(grad.shape[0], n, -1), (1, 0, 2))
    return lax.psum_scatter(parts, "dp", scatter_dimension=0, tiled=False).astype(F32)


def body(
    layer_input,
    row_seq,
    qkv_weight,
    out_weight,
    in_weight,
    down_weight,
    attn_gain,
    mlp_gain,
    cotangent,
):
    me = lax.axis_index("mp")
    me_arg = me.reshape(1).astype(jnp.int32)
    share, model = layer_input.shape
    width = qkv_weight.shape[2]
    units = in_weight.shape[2]
    gains = lax.all_gather(jnp.stack([attn_gain, mlp_gain]), "dp", axis=0)
    gains = jnp.transpose(gains, (1, 0, 2)).reshape(2, model).astype(F32)
    gain_one, gain_two = (gains[0], gains[1])
    w_qkv = lax.all_gather(qkv_weight.reshape(-1, 3 * width), "dp", axis=0, tiled=True)
    w_out = gather_columns(out_weight)
    w_in = lax.all_gather(in_weight.reshape(-1, 2 * units), "dp", axis=0, tiled=True)
    w_gate, w_up = (w_in[:, :units], w_in[:, units:])
    w_down = gather_columns(down_weight)

    quarters = jnp.stack(spread(row_seq))
    seq_all = jnp.take(quarters, jnp.arange(4) ^ me, axis=0).reshape(-1)
    group_rows = seq_all.shape[0]
    blocks = group_rows // WIN
    cosine, sine = rotation_tables(positions(seq_all))
    padded_seq = jnp.pad(seq_all, (WIN // 2, WIN // 2), constant_values=-5).reshape(-1, WIN)
    seq_rows = jnp.concatenate([padded_seq[:-1], padded_seq[1:]], axis=1).reshape(
        blocks, 1, 2 * WIN
    )
    tables = (cosine, sine, seq_all[:, None], seq_rows)

    grad_final = cotangent.astype(F32) * (row_seq >= 0).astype(F32)[:, None]
    grad_all = jnp.concatenate(spread(grad_final.astype(BF16)), axis=0)

    block_in = layer_input.astype(F32)
    normed_one, factor_one = normalize(block_in)
    h_all = jnp.concatenate(spread((normed_one * gain_one).astype(BF16)), axis=0)
    qkv = jnp.dot(h_all, w_qkv, preferred_element_type=F32)
    mixed, queries, keys, values = attend_forward(
        me_arg, qkv.reshape(4, share, 3 * width), tables, width
    )
    middle = block_in + collect(
        lambda r: jnp.dot(mixed[r], w_out, preferred_element_type=F32)
    )
    normed_two, factor_two = normalize(middle)
    h2_parts = spread((normed_two * gain_two).astype(BF16))
    h2_all = jnp.concatenate(h2_parts, axis=0)
    gate_vals = jnp.dot(h2_all, w_gate, preferred_element_type=F32)
    up_values = jnp.dot(h2_all, w_up, preferred_element_type=F32)
    hidden = (jax.nn.gelu(gate_vals, approximate=False) * up_values).astype(BF16)

    def quarter_of(tensor, r):
        return lax.slice_in_dim(tensor, r * share, (r + 1) * share, axis=0)

    final_rows = middle + collect(
        lambda r: jnp.dot(quarter_of(hidden, r), w_down, preferred_element_type=F32)
    )
    activations = final_rows.astype(BF16)

    down_share = scatter_columns(dot_tn(hidden, grad_all))
    grad_hidden = dot_nt(grad_all, w_down)

    def product(gate_in, up_in):
        return jax.nn.gelu(gate_in, approximate=False) * up_in

    _, pullback = jax.vjp(product, gate_vals, up_values)
    grad_gate, grad_up = (item.astype(BF16) for item in pullback(grad_hidden))
    grad_h_two = collect(
        lambda r: dot_nt(quarter_of(grad_gate, r), w_gate) + dot_nt(quarter_of(grad_up, r), w_up)
    )
    grad_norm_two, gain_two_grad = norm_back(grad_h_two, normed_two, factor_two, gain_two)
    grad_middle = grad_final + grad_norm_two
    grad_mid_all = jnp.concatenate(spread(grad_middle.astype(BF16)), axis=0)
    in_share = scatter_rows(
        jnp.concatenate([dot_tn(h2_all, grad_gate), dot_tn(h2_all, grad_up)], axis=1)
    ).reshape(-1, 2, units)
    grad_mixed = dot_nt(grad_mid_all, w_out).astype(BF16).reshape(4, share, width)
    grad_qkv = attend_backward(me_arg, queries, keys, values, grad_mixed, tables)
    out_share = scatter_columns(dot_tn(mixed.reshape(group_rows, width), grad_mid_all))
    grad_h_one = collect(lambda r: dot_nt(grad_qkv[r], w_qkv))
    grad_norm_one, gain_one_grad = norm_back(grad_h_one, normed_one, factor_one, gain_one)
    input_grad = (grad_middle + grad_norm_one).astype(BF16)
    qkv_share = scatter_rows(dot_tn(h_all, grad_qkv.reshape(group_rows, 3 * width))).reshape(
        -1, 3, width
    )
    gain_total = lax.psum(jnp.stack([gain_one_grad, gain_two_grad]), ("dp", "mp"))
    own = attn_gain.shape[0]
    gain_total = lax.dynamic_slice_in_dim(gain_total, lax.axis_index("dp") * own, own, 1)
    return (
        activations,
        input_grad,
        gain_total[0],
        gain_total[1],
        qkv_share,
        out_share,
        in_share,
        down_share,
    )


def solution(mesh):
    in_specs = (
        P(("dp", "mp"), None),
        P(("dp", "mp")),
        P("dp", None, "mp"),
        P("mp", "dp"),
        P("dp", None, "mp"),
        P("mp", "dp"),
        P("dp"),
        P("dp"),
        P(("dp", "mp"), None),
    )
    out_specs = (
        P(("dp", "mp"), None),
        P(("dp", "mp"), None),
        P("dp"),
        P("dp"),
        P("dp", None, "mp"),
        P("mp", "dp"),
        P("dp", None, "mp"),
        P("mp", "dp"),
    )
    return jax.shard_map(body, mesh=mesh, in_specs=in_specs, out_specs=out_specs, check_vma=False)
```

```python
import math

import jax
import jax.numpy as jnp
from jax import lax
from jax.experimental import pallas as pl
from jax.experimental.pallas import tpu as pltpu
from jax.sharding import PartitionSpec as P

HEAD_DIM = 64
WIN = 128
EPSILON = 1e-05
THETA_BASE = 10000.0
BF16 = jnp.bfloat16
F32 = jnp.float32


def normalize(block_in):
    row_mean = jnp.mean(block_in, axis=-1, keepdims=True)
    centred = block_in - row_mean
    variance = jnp.mean(centred * centred, axis=-1, keepdims=True)
    factor = lax.rsqrt(variance + EPSILON)
    return (centred * factor, factor)


def norm_back(grad_in, normed, factor, gain):
    scaled = grad_in * gain
    centred_grad = (
        scaled
        - jnp.mean(scaled, axis=-1, keepdims=True)
        - normed * jnp.mean(scaled * normed, axis=-1, keepdims=True)
    )
    return (factor * centred_grad, jnp.sum(grad_in * normed, axis=0))


def positions(sequence):
    length = sequence.shape[0]
    row_index = jnp.arange(length, dtype=jnp.int32)
    before = jnp.concatenate([jnp.full((1,), -7, jnp.int32), sequence[:-1]])
    run_start = lax.cummax(jnp.where(sequence != before, row_index, 0), axis=0)
    return row_index - run_start


def rotation_tables(place):
    half = HEAD_DIM // 2
    frequency = jnp.exp(
        jnp.arange(half, dtype=F32) * (-2.0 * math.log(THETA_BASE) / HEAD_DIM)
    )
    angles = place.astype(F32)[:, None] * frequency[None, :]
    cosine, sine = (jnp.cos(angles), jnp.sin(angles))
    return (
        jnp.concatenate([cosine] * 4, axis=1),
        jnp.concatenate([-sine, sine, -sine, sine], axis=1),
    )


def turn(tensor, cosine, signed_sine):
    lane = lax.broadcasted_iota(jnp.int32, cosine.shape, 1)
    first = (lane % HEAD_DIM) < HEAD_DIM // 2
    parts = []
    for start in range(0, tensor.shape[1], 128):
        piece = tensor[:, start : start + 128]
        other = jnp.where(first, pltpu.roll(piece, 96, 1), pltpu.roll(piece, 32, 1))
        parts.append(piece * cosine + other * signed_sine)
    return jnp.concatenate(parts, axis=1)


def head_masks(heads, width):
    lane = lax.broadcasted_iota(jnp.int32, (WIN, width), 1)
    return [(lane // HEAD_DIM == head).astype(F32) for head in range(heads)]


def allowed_pairs(seq_col, seq_row):
    query = lax.broadcasted_iota(jnp.int32, (WIN, 2 * WIN), 0) + WIN // 2
    key = lax.broadcasted_iota(jnp.int32, (WIN, 2 * WIN), 1)
    distance = jnp.abs(query - key)
    same_run = (seq_col == seq_row) & (seq_col >= 0) & (distance <= WIN // 2)
    return same_run | (distance == 0)


def place_of(block, me, per_quarter):
    quarter = lax.div(block, per_quarter)
    start = pl.multiple_of(lax.rem(block, per_quarter) * WIN, WIN)
    return (jnp.bitwise_xor(quarter, me), pl.ds(start, WIN))


def probabilities_of(queries, keys, allowed, masks):
    heads = len(masks)
    stacked = jnp.concatenate([queries * mask.astype(BF16) for mask in masks], axis=0)
    scores = lax.dot_general(
        stacked, keys, (((1,), (1,)), ((), ())), preferred_element_type=F32
    ) * (1.0 / math.sqrt(HEAD_DIM))
    scores = scores.reshape(heads, WIN, 2 * WIN)
    scores = jnp.where(allowed[None], scores, -1e30)
    weights = jnp.exp(scores - jnp.max(scores, axis=-1, keepdims=True))
    total = jnp.sum(weights, axis=-1, keepdims=True)
    return (stacked, weights * (1.0 / total))


def forward_kernel(
    me_ref, qi_ref, ki_ref, vi_ref, cos_ref, sin_ref, col_ref, row_ref, o_ref, q_ref, k_ref, v_ref
):
    me = me_ref[0]
    rows, width = q_ref.shape
    blocks = rows // WIN
    per_quarter = qi_ref.shape[1] // WIN
    half = WIN // 2
    for ref in (k_ref, v_ref):
        ref[0:half, :] = jnp.zeros((half, width), BF16)
        ref[rows + half : rows + 2 * half, :] = jnp.zeros((half, width), BF16)

    def turn_block(block, carry):
        quarter, inner = place_of(block, me, per_quarter)
        start = pl.multiple_of(block * WIN, WIN)
        here = pl.ds(start, WIN)
        later = pl.ds(pl.multiple_of(start + half, half), WIN)
        cosine, sine = (cos_ref[here, :], sin_ref[here, :])
        q_ref[here, :] = turn(qi_ref[quarter, inner, :], cosine, sine).astype(BF16)
        k_ref[later, :] = turn(ki_ref[quarter, inner, :], cosine, sine).astype(BF16)
        v_ref[later, :] = vi_ref[quarter, inner, :].astype(BF16)
        return carry

    lax.fori_loop(0, blocks, turn_block, 0)
    masks = head_masks(width // HEAD_DIM, width)

    def attend_block(block, carry):
        quarter, inner = place_of(block, me, per_quarter)
        start = pl.multiple_of(block * WIN, WIN)
        span = pl.ds(start, 2 * WIN)
        allowed = allowed_pairs(col_ref[pl.ds(start, WIN), :], row_ref[block])
        _, prob = probabilities_of(q_ref[pl.ds(start, WIN), :], k_ref[span, :], allowed, masks)
        prob = prob.astype(BF16).reshape(-1, 2 * WIN)
        mixed = jnp.dot(prob, v_ref[span, :], preferred_element_type=F32)
        mixed = mixed.reshape(len(masks), WIN, width)
        o_ref[quarter, inner, :] = sum(
            mixed[head] * mask for head, mask in enumerate(masks)
        ).astype(BF16)
        return carry

    lax.fori_loop(0, blocks, attend_block, 0)


def backward_kernel(
    me_ref, q_ref, k_ref, v_ref, g_ref, cos_ref, sin_ref, col_ref, row_ref, d_ref, dk_ref, dv_ref
):
    me = me_ref[0]
    rows, width = q_ref.shape
    blocks = rows // WIN
    per_quarter = g_ref.shape[1] // WIN
    half = WIN // 2
    factor = 1.0 / math.sqrt(HEAD_DIM)
    dk_ref[...] = jnp.zeros(dk_ref.shape, F32)
    dv_ref[...] = jnp.zeros(dv_ref.shape, F32)
    masks = head_masks(width // HEAD_DIM, width)
    over_rows = (((0,), (0,)), ((), ()))

    def attend_block(block, carry):
        quarter, inner = place_of(block, me, per_quarter)
        start = pl.multiple_of(block * WIN, WIN)
        here = pl.ds(start, WIN)
        span = pl.ds(start, 2 * WIN)
        allowed = allowed_pairs(col_ref[here, :], row_ref[block])
        keys = k_ref[span, :]
        queries, prob = probabilities_of(q_ref[here, :], keys, allowed, masks)
        grads = g_ref[quarter, inner, :]
        grads = jnp.concatenate([grads * mask.astype(BF16) for mask in masks], axis=0)
        grad_prob = lax.dot_general(
            grads, v_ref[span, :], (((1,), (1,)), ((), ())), preferred_element_type=F32
        ).reshape(prob.shape)
        inner_sum = jnp.sum(prob * grad_prob, axis=-1, keepdims=True)
        grad_score = (prob * (grad_prob - inner_sum)).astype(BF16).reshape(-1, 2 * WIN)
        prob = prob.astype(BF16).reshape(-1, 2 * WIN)
        dv_ref[span, :] += lax.dot_general(prob, grads, over_rows, preferred_element_type=F32)
        dk_ref[span, :] += lax.dot_general(
            grad_score, queries, over_rows, preferred_element_type=F32
        )
        grad_query = jnp.dot(grad_score, keys, preferred_element_type=F32)
        grad_query = grad_query.reshape(len(masks), WIN, width)
        grad_query = sum(grad_query[head] * mask for head, mask in enumerate(masks)) * factor
        d_ref[quarter, inner, 0:width] = turn(
            grad_query, cos_ref[here, :], -sin_ref[here, :]
        ).astype(BF16)
        return carry

    lax.fori_loop(0, blocks, attend_block, 0)

    def finish_block(block, carry):
        quarter, inner = place_of(block, me, per_quarter)
        start = pl.multiple_of(block * WIN, WIN)
        here = pl.ds(start, WIN)
        later = pl.ds(pl.multiple_of(start + half, half), WIN)
        d_ref[quarter, inner, width : 2 * width] = turn(
            dk_ref[later, :] * factor, cos_ref[here, :], -sin_ref[here, :]
        ).astype(BF16)
        d_ref[quarter, inner, 2 * width : 3 * width] = dv_ref[later, :].astype(BF16)
        return carry

    lax.fori_loop(0, blocks, finish_block, 0)


def vmem_specs(count):
    return [pl.BlockSpec(memory_space=pltpu.SMEM)] + [pl.BlockSpec(memory_space=pltpu.VMEM)] * count


def attend_forward(me, qkv, tables):
    quarters, share, width = qkv[0].shape
    rows = quarters * share
    padded = jax.ShapeDtypeStruct((rows + WIN, width), BF16)
    return pl.pallas_call(
        forward_kernel,
        out_shape=(
            jax.ShapeDtypeStruct((quarters, share, width), BF16),
            jax.ShapeDtypeStruct((rows, width), BF16),
            padded,
            padded,
        ),
        in_specs=vmem_specs(7),
        out_specs=(pl.BlockSpec(memory_space=pltpu.VMEM),) * 4,
        compiler_params=pltpu.CompilerParams(vmem_limit_bytes=40 * 2**20),
        cost_estimate=pl.CostEstimate(
            flops=16 * rows * WIN * width, bytes_accessed=16 * rows * width, transcendentals=0
        ),
        name="attend_forward",
    )(me, *qkv, *tables)


def attend_backward(me, queries, keys, values, grads, tables):
    quarters, share, width = grads.shape
    rows = quarters * share
    accumulator = pltpu.VMEM((rows + WIN, width), F32)
    return pl.pallas_call(
        backward_kernel,
        out_shape=jax.ShapeDtypeStruct((quarters, share, 3 * width), BF16),
        in_specs=vmem_specs(8),
        out_specs=pl.BlockSpec(memory_space=pltpu.VMEM),
        scratch_shapes=[accumulator, accumulator],
        compiler_params=pltpu.CompilerParams(vmem_limit_bytes=40 * 2**20),
        cost_estimate=pl.CostEstimate(
            flops=40 * rows * WIN * width, bytes_accessed=16 * rows * width, transcendentals=0
        ),
        name="attend_backward",
    )(me, queries, keys, values, grads, *tables)


def swap(tensor, bit):
    return lax.ppermute(tensor, "mp", [(i, i ^ bit) for i in range(4)])


def spread(rows):
    across = swap(rows, 2)
    return [rows, swap(rows, 1), across, swap(across, 1)]


def collect(product):
    away = [swap(product(r).astype(BF16), 1) for r in (3, 1)]
    across = swap((product(2) + away[0].astype(F32)).astype(BF16), 2)
    return product(0) + away[1].astype(F32) + across.astype(F32)


def dot_nt(left, right):
    return lax.dot_general(left, right, (((1,), (1,)), ((), ())), preferred_element_type=F32)


def dot_tn(left, right):
    return lax.dot_general(left, right, (((0,), (0,)), ((), ())), preferred_element_type=F32)


def pairs(bit):
    return [(i, i ^ bit) for i in range(lax.axis_size("dp"))]


def dp_bits():
    bits = []
    while 2 ** len(bits) < lax.axis_size("dp"):
        bits.insert(0, 2 ** len(bits))
    return bits


def my_bit(bit):
    return (lax.axis_index("dp") & bit) != 0


def first_doublings(shard):
    held = shard
    for step, bit in enumerate(dp_bits()[:-1]):
        held = doubling(held, step, bit)
    return held


def doubling(held, step, bit):
    other = lax.ppermute(held, "dp", pairs(bit))
    upper = my_bit(bit)
    return jnp.stack(
        [jnp.where(upper, other, held), jnp.where(upper, held, other)], axis=step
    )


def last_doubling(held, shard_shape):
    bits = dp_bits()
    return doubling(held, len(bits) - 1, bits[-1]).reshape((-1,) + shard_shape)


def halving(parts):
    bits = dp_bits()
    held = parts.reshape((2,) * len(bits) + parts.shape[1:])
    for step in reversed(range(len(bits))):
        mine = my_bit(bits[step]).astype(jnp.int32)
        away = lax.dynamic_index_in_dim(held, 1 - mine, axis=step, keepdims=False)
        kept = lax.dynamic_index_in_dim(held, mine, axis=step, keepdims=False)
        arrived = lax.ppermute(away, "dp", pairs(bits[step]))
        held = (kept.astype(F32) + arrived.astype(F32)).astype(
            parts.dtype if step else F32
        )
    return held


def merge_rows(parts):
    return parts.reshape((-1,) + parts.shape[2:])


def merge_columns(parts):
    return jnp.transpose(parts, (1, 0, 2)).reshape(parts.shape[1], -1)


def scatter_rows(grad):
    return halving(grad.astype(BF16).reshape(lax.axis_size("dp"), -1, grad.shape[1]))


def scatter_columns(grad):
    parts = grad.astype(BF16).reshape(grad.shape[0], lax.axis_size("dp"), -1)
    return halving(jnp.transpose(parts, (1, 0, 2)))


def body(
    layer_input,
    row_seq,
    qkv_weight,
    out_weight,
    in_weight,
    down_weight,
    attn_gain,
    mlp_gain,
    cotangent,
):
    me = lax.axis_index("mp")
    me_arg = me.reshape(1).astype(jnp.int32)
    share, model = layer_input.shape
    width = qkv_weight.shape[2]
    units = in_weight.shape[2]
    gain_shape = (2,) + attn_gain.shape
    gains = last_doubling(first_doublings(jnp.stack([attn_gain, mlp_gain])), gain_shape)
    gains = merge_columns(gains).astype(F32)
    gain_one, gain_two = (gains[0], gains[1])
    x_parts = spread(layer_input)
    projections = [first_doublings(qkv_weight[:, part]) for part in range(3)]
    late = [out_weight, in_weight[:, 0], in_weight[:, 1], down_weight]
    *late, projections[2] = lax.optimization_barrier((*late, projections[2]))
    w_q, w_k, w_v = [
        merge_rows(last_doubling(item, (qkv_weight.shape[0], width))) for item in projections
    ]
    late = [last_doubling(first_doublings(item), item.shape) for item in late]
    w_out, w_down = (merge_columns(late[0]), merge_columns(late[3]))
    w_gate, w_up = (merge_rows(late[1]), merge_rows(late[2]))
    w_qkv = jnp.concatenate([w_q, w_k, w_v], axis=1)

    quarters = jnp.stack(spread(row_seq))
    seq_all = jnp.take(quarters, jnp.arange(4) ^ me, axis=0).reshape(-1)
    group_rows = seq_all.shape[0]
    blocks = group_rows // WIN
    cosine, sine = rotation_tables(positions(seq_all))
    padded_seq = jnp.pad(seq_all, (WIN // 2, WIN // 2), constant_values=-5).reshape(-1, WIN)
    seq_rows = jnp.concatenate([padded_seq[:-1], padded_seq[1:]], axis=1).reshape(
        blocks, 1, 2 * WIN
    )
    tables = (cosine, sine, seq_all[:, None], seq_rows)

    grad_final = cotangent.astype(F32) * (row_seq >= 0).astype(F32)[:, None]
    grad_parts = spread(grad_final.astype(BF16))

    block_in = layer_input.astype(F32)
    normed_one, factor_one = normalize(block_in)
    h_all = (normalize(jnp.concatenate(x_parts, axis=0).astype(F32))[0] * gain_one).astype(BF16)
    qkv = [
        jnp.dot(h_all, part, preferred_element_type=F32).reshape(4, share, width)
        for part in (w_q, w_k, w_v)
    ]
    grad_parts, qkv = lax.optimization_barrier((grad_parts, qkv))
    mixed, queries, keys, values = attend_forward(me_arg, qkv, tables)
    middle = block_in + collect(
        lambda r: jnp.dot(mixed[r], w_out, preferred_element_type=F32)
    )
    normed_two, factor_two = normalize(middle)
    h2_parts = spread((normed_two * gain_two).astype(BF16))

    def product(gate_in, up_in):
        return jax.nn.gelu(gate_in, approximate=False) * up_in

    halves = []
    for start in (0, 2):
        h_rows = jnp.concatenate(h2_parts[start : start + 2], axis=0)
        g_rows = jnp.concatenate(grad_parts[start : start + 2], axis=0)
        gate_vals = jnp.dot(h_rows, w_gate, preferred_element_type=F32)
        up_values = jnp.dot(h_rows, w_up, preferred_element_type=F32)
        value, pullback = jax.vjp(product, gate_vals, up_values)
        grad_gate, grad_up = pullback(dot_nt(g_rows, w_down))
        halves.append(
            (h_rows, g_rows, value.astype(BF16), grad_gate.astype(BF16), grad_up.astype(BF16))
        )

    def quarter_of(part, r):
        return halves[r // 2][part][(r % 2) * share : (r % 2 + 1) * share]

    grad_h_two = collect(
        lambda r: dot_nt(quarter_of(3, r), w_gate) + dot_nt(quarter_of(4, r), w_up)
    )
    h2_all, grad_all, hidden, grad_gate, grad_up = [
        jnp.concatenate(pair, axis=0) for pair in zip(*halves)
    ]
    down_share = scatter_columns(dot_tn(hidden, grad_all))
    in_share = jnp.stack(
        [scatter_rows(dot_tn(h2_all, grad_gate)), scatter_rows(dot_tn(h2_all, grad_up))], axis=1
    )
    grad_norm_two, gain_two_grad = norm_back(grad_h_two, normed_two, factor_two, gain_two)
    grad_middle = grad_final + grad_norm_two
    grad_mid_own, late_hidden = lax.optimization_barrier(
        (grad_middle.astype(BF16), [item[2] for item in halves])
    )
    grad_mid_all = jnp.concatenate(spread(grad_mid_own), axis=0)
    activations = (
        middle
        + collect(
            lambda r: jnp.dot(
                late_hidden[r // 2][(r % 2) * share : (r % 2 + 1) * share],
                w_down,
                preferred_element_type=F32,
            )
        )
    ).astype(BF16)
    grad_mixed = dot_nt(grad_mid_all, w_out).astype(BF16).reshape(4, share, width)
    grad_qkv = attend_backward(me_arg, queries, keys, values, grad_mixed, tables)
    out_share = scatter_columns(dot_tn(mixed.reshape(group_rows, width), grad_mid_all))
    grad_h_one = collect(lambda r: dot_nt(grad_qkv[r], w_qkv))
    grad_norm_one, gain_one_grad = norm_back(grad_h_one, normed_one, factor_one, gain_one)
    input_grad = (grad_middle + grad_norm_one).astype(BF16)
    flat_grad = grad_qkv.reshape(group_rows, 3 * width)
    qkv_share = jnp.stack(
        [
            scatter_rows(dot_tn(h_all, flat_grad[:, part * width : (part + 1) * width]))
            for part in range(3)
        ],
        axis=1,
    )
    gain_total = jnp.stack([gain_one_grad, gain_two_grad]).reshape(2, lax.axis_size("dp"), -1)
    gain_total = halving(jnp.transpose(gain_total, (1, 0, 2)))
    for bit in (1, 2):
        gain_total = gain_total + swap(gain_total, bit)
    return (
        activations,
        input_grad,
        gain_total[0],
        gain_total[1],
        qkv_share,
        out_share,
        in_share,
        down_share,
    )


def solution(mesh):
    in_specs = (
        P(("dp", "mp"), None),
        P(("dp", "mp")),
        P("dp", None, "mp"),
        P("mp", "dp"),
        P("dp", None, "mp"),
        P("mp", "dp"),
        P("dp"),
        P("dp"),
        P(("dp", "mp"), None),
    )
    out_specs = (
        P(("dp", "mp"), None),
        P(("dp", "mp"), None),
        P("dp"),
        P("dp"),
        P("dp", None, "mp"),
        P("mp", "dp"),
        P("dp", None, "mp"),
        P("mp", "dp"),
    )
    return jax.shard_map(body, mesh=mesh, in_specs=in_specs, out_specs=out_specs, check_vma=False)
```

```python
import functools
import math

import jax
import jax.numpy as jnp
from jax import lax
from jax.experimental import pallas as pl
from jax.experimental.pallas import tpu as pltpu
from jax.sharding import PartitionSpec as P

HEAD_DIM = 64
WIN = 128
EPSILON = 1e-05
THETA_BASE = 10000.0
BF16 = jnp.bfloat16
MESH = pl.DeviceIdType.MESH
F32 = jnp.float32


def normalize(block_in):
    row_mean = jnp.mean(block_in, axis=-1, keepdims=True)
    centred = block_in - row_mean
    variance = jnp.mean(centred * centred, axis=-1, keepdims=True)
    factor = lax.rsqrt(variance + EPSILON)
    return (centred * factor, factor)


def norm_back(grad_in, normed, factor, gain):
    scaled = grad_in * gain
    centred_grad = (
        scaled
        - jnp.mean(scaled, axis=-1, keepdims=True)
        - normed * jnp.mean(scaled * normed, axis=-1, keepdims=True)
    )
    return (factor * centred_grad, jnp.sum(grad_in * normed, axis=0))


def positions(sequence):
    length = sequence.shape[0]
    row_index = jnp.arange(length, dtype=jnp.int32)
    before = jnp.concatenate([jnp.full((1,), -7, jnp.int32), sequence[:-1]])
    run_start = lax.cummax(jnp.where(sequence != before, row_index, 0), axis=0)
    return row_index - run_start


def rotation_tables(place):
    half = HEAD_DIM // 2
    frequency = jnp.exp(
        jnp.arange(half, dtype=F32) * (-2.0 * math.log(THETA_BASE) / HEAD_DIM)
    )
    angles = place.astype(F32)[:, None] * frequency[None, :]
    cosine, sine = (jnp.cos(angles), jnp.sin(angles))
    return (
        jnp.concatenate([cosine] * 4, axis=1),
        jnp.concatenate([-sine, sine, -sine, sine], axis=1),
    )


def turn(tensor, cosine, signed_sine):
    lane = lax.broadcasted_iota(jnp.int32, cosine.shape, 1)
    first = (lane % HEAD_DIM) < HEAD_DIM // 2
    parts = []
    for start in range(0, tensor.shape[1], 128):
        piece = tensor[:, start : start + 128]
        other = jnp.where(first, pltpu.roll(piece, 96, 1), pltpu.roll(piece, 32, 1))
        parts.append(piece * cosine + other * signed_sine)
    return jnp.concatenate(parts, axis=1)


def head_masks(heads, width):
    lane = lax.broadcasted_iota(jnp.int32, (WIN, width), 1)
    return [(lane // HEAD_DIM == head).astype(F32) for head in range(heads)]


def allowed_pairs(seq_col, seq_row):
    query = lax.broadcasted_iota(jnp.int32, (WIN, 2 * WIN), 0) + WIN // 2
    key = lax.broadcasted_iota(jnp.int32, (WIN, 2 * WIN), 1)
    distance = jnp.abs(query - key)
    same_run = (seq_col == seq_row) & (seq_col >= 0) & (distance <= WIN // 2)
    return same_run | (distance == 0)


def place_of(block, me, per_quarter):
    quarter = lax.div(block, per_quarter)
    start = pl.multiple_of(lax.rem(block, per_quarter) * WIN, WIN)
    return (jnp.bitwise_xor(quarter, me), pl.ds(start, WIN))


def probabilities_of(queries, keys, allowed, masks):
    heads = len(masks)
    stacked = jnp.concatenate([queries * mask.astype(BF16) for mask in masks], axis=0)
    scores = lax.dot_general(
        stacked, keys, (((1,), (1,)), ((), ())), preferred_element_type=F32
    ) * (1.0 / math.sqrt(HEAD_DIM))
    scores = scores.reshape(heads, WIN, 2 * WIN)
    scores = jnp.where(allowed[None], scores, -1e30)
    weights = jnp.exp(scores - jnp.max(scores, axis=-1, keepdims=True))
    total = jnp.sum(weights, axis=-1, keepdims=True)
    return (stacked, weights * (1.0 / total))


def forward_kernel(
    me_ref, qi_ref, ki_ref, vi_ref, cos_ref, sin_ref, col_ref, row_ref, o_ref, q_ref, k_ref, v_ref
):
    me = me_ref[0]
    rows, width = q_ref.shape
    blocks = rows // WIN
    per_quarter = qi_ref.shape[1] // WIN
    half = WIN // 2
    for ref in (k_ref, v_ref):
        ref[0:half, :] = jnp.zeros((half, width), BF16)
        ref[rows + half : rows + 2 * half, :] = jnp.zeros((half, width), BF16)

    def turn_block(block, carry):
        quarter, inner = place_of(block, me, per_quarter)
        start = pl.multiple_of(block * WIN, WIN)
        here = pl.ds(start, WIN)
        later = pl.ds(pl.multiple_of(start + half, half), WIN)
        cosine, sine = (cos_ref[here, :], sin_ref[here, :])
        q_ref[here, :] = turn(qi_ref[quarter, inner, :], cosine, sine).astype(BF16)
        k_ref[later, :] = turn(ki_ref[quarter, inner, :], cosine, sine).astype(BF16)
        v_ref[later, :] = vi_ref[quarter, inner, :].astype(BF16)
        return carry

    lax.fori_loop(0, blocks, turn_block, 0)
    masks = head_masks(width // HEAD_DIM, width)

    def attend_block(block, carry):
        quarter, inner = place_of(block, me, per_quarter)
        start = pl.multiple_of(block * WIN, WIN)
        span = pl.ds(start, 2 * WIN)
        allowed = allowed_pairs(col_ref[pl.ds(start, WIN), :], row_ref[block])
        _, prob = probabilities_of(q_ref[pl.ds(start, WIN), :], k_ref[span, :], allowed, masks)
        prob = prob.astype(BF16).reshape(-1, 2 * WIN)
        mixed = jnp.dot(prob, v_ref[span, :], preferred_element_type=F32)
        mixed = mixed.reshape(len(masks), WIN, width)
        o_ref[quarter, inner, :] = sum(
            mixed[head] * mask for head, mask in enumerate(masks)
        ).astype(BF16)
        return carry

    lax.fori_loop(0, blocks, attend_block, 0)


def backward_kernel(
    me_ref, q_ref, k_ref, v_ref, g_ref, cos_ref, sin_ref, col_ref, row_ref, d_ref, dk_ref, dv_ref
):
    me = me_ref[0]
    rows, width = q_ref.shape
    blocks = rows // WIN
    per_quarter = g_ref.shape[1] // WIN
    half = WIN // 2
    factor = 1.0 / math.sqrt(HEAD_DIM)
    dk_ref[...] = jnp.zeros(dk_ref.shape, F32)
    dv_ref[...] = jnp.zeros(dv_ref.shape, F32)
    masks = head_masks(width // HEAD_DIM, width)
    over_rows = (((0,), (0,)), ((), ()))

    def attend_block(block, carry):
        quarter, inner = place_of(block, me, per_quarter)
        start = pl.multiple_of(block * WIN, WIN)
        here = pl.ds(start, WIN)
        span = pl.ds(start, 2 * WIN)
        allowed = allowed_pairs(col_ref[here, :], row_ref[block])
        keys = k_ref[span, :]
        queries, prob = probabilities_of(q_ref[here, :], keys, allowed, masks)
        grads = g_ref[quarter, inner, :]
        grads = jnp.concatenate([grads * mask.astype(BF16) for mask in masks], axis=0)
        grad_prob = lax.dot_general(
            grads, v_ref[span, :], (((1,), (1,)), ((), ())), preferred_element_type=F32
        ).reshape(prob.shape)
        inner_sum = jnp.sum(prob * grad_prob, axis=-1, keepdims=True)
        grad_score = (prob * (grad_prob - inner_sum)).astype(BF16).reshape(-1, 2 * WIN)
        prob = prob.astype(BF16).reshape(-1, 2 * WIN)
        dv_ref[span, :] += lax.dot_general(prob, grads, over_rows, preferred_element_type=F32)
        dk_ref[span, :] += lax.dot_general(
            grad_score, queries, over_rows, preferred_element_type=F32
        )
        grad_query = jnp.dot(grad_score, keys, preferred_element_type=F32)
        grad_query = grad_query.reshape(len(masks), WIN, width)
        grad_query = sum(grad_query[head] * mask for head, mask in enumerate(masks)) * factor
        d_ref[quarter, inner, 0:width] = turn(
            grad_query, cos_ref[here, :], -sin_ref[here, :]
        ).astype(BF16)
        return carry

    lax.fori_loop(0, blocks, attend_block, 0)

    def finish_block(block, carry):
        quarter, inner = place_of(block, me, per_quarter)
        start = pl.multiple_of(block * WIN, WIN)
        here = pl.ds(start, WIN)
        later = pl.ds(pl.multiple_of(start + half, half), WIN)
        d_ref[quarter, inner, width : 2 * width] = turn(
            dk_ref[later, :] * factor, cos_ref[here, :], -sin_ref[here, :]
        ).astype(BF16)
        d_ref[quarter, inner, 2 * width : 3 * width] = dv_ref[later, :].astype(BF16)
        return carry

    lax.fori_loop(0, blocks, finish_block, 0)


def vmem_specs(count):
    return [pl.BlockSpec(memory_space=pltpu.SMEM)] + [pl.BlockSpec(memory_space=pltpu.VMEM)] * count


def attend_forward(me, qkv, tables):
    quarters, share, width = qkv[0].shape
    rows = quarters * share
    padded = jax.ShapeDtypeStruct((rows + WIN, width), BF16)
    return pl.pallas_call(
        forward_kernel,
        out_shape=(
            jax.ShapeDtypeStruct((quarters, share, width), BF16),
            jax.ShapeDtypeStruct((rows, width), BF16),
            padded,
            padded,
        ),
        in_specs=vmem_specs(7),
        out_specs=(pl.BlockSpec(memory_space=pltpu.VMEM),) * 4,
        compiler_params=pltpu.CompilerParams(vmem_limit_bytes=40 * 2**20),
        cost_estimate=pl.CostEstimate(
            flops=16 * rows * WIN * width, bytes_accessed=16 * rows * width, transcendentals=0
        ),
        name="attend_forward",
    )(me, *qkv, *tables)


def attend_backward(me, queries, keys, values, grads, tables):
    quarters, share, width = grads.shape
    rows = quarters * share
    accumulator = pltpu.VMEM((rows + WIN, width), F32)
    return pl.pallas_call(
        backward_kernel,
        out_shape=jax.ShapeDtypeStruct((quarters, share, 3 * width), BF16),
        in_specs=vmem_specs(8),
        out_specs=pl.BlockSpec(memory_space=pltpu.VMEM),
        scratch_shapes=[accumulator, accumulator],
        compiler_params=pltpu.CompilerParams(vmem_limit_bytes=40 * 2**20),
        cost_estimate=pl.CostEstimate(
            flops=40 * rows * WIN * width, bytes_accessed=16 * rows * width, transcendentals=0
        ),
        name="attend_backward",
    )(me, queries, keys, values, grads, *tables)


def swap(tensor, bit):
    return lax.ppermute(tensor, "mp", [(i, i ^ bit) for i in range(4)])


def spread(rows):
    across = swap(rows, 2)
    return [rows, swap(rows, 1), across, swap(across, 1)]


def collect(product):
    away = [swap(product(r).astype(BF16), 1) for r in (3, 1)]
    across = swap((product(2) + away[0].astype(F32)).astype(BF16), 2)
    return product(0) + away[1].astype(F32) + across.astype(F32)


def dot_nt(left, right):
    return lax.dot_general(left, right, (((1,), (1,)), ((), ())), preferred_element_type=F32)


def dot_tn(left, right):
    return lax.dot_general(left, right, (((0,), (0,)), ((), ())), preferred_element_type=F32)


def bits_of(count):
    return [2**place for place in range(count.bit_length() - 1)]


def lowest(value):
    return value & -value


def greet(n, me, mp):
    barrier = pltpu.get_barrier_semaphore()
    partners = [{"dp": jnp.bitwise_xor(me, bit)} for bit in bits_of(n)]
    partners += [{"mp": jnp.bitwise_xor(mp, bit)} for bit in (1, 2)]
    for partner in partners:
        pl.semaphore_signal(barrier, inc=1, device_id=partner, device_id_type=MESH)
    pl.semaphore_wait(barrier, len(partners))


def remote(source, target, send_sem, recv_sem, axis, device):
    return pltpu.make_async_remote_copy(
        src_ref=source,
        dst_ref=target,
        send_sem=send_sem,
        recv_sem=recv_sem,
        device_id={axis: device},
        device_id_type=MESH,
    )


def gather_kernel(
    n, w_ref, g_ref, x_ref, wo_ref, go_ref, xo_ref, dp_send, dp_recv, mp_send, mp_recv
):
    me, mp = (lax.axis_index("dp"), lax.axis_index("mp"))
    greet(n, me, mp)
    pairs = ((w_ref, wo_ref), (g_ref, go_ref))
    bits = bits_of(n)[::-1]
    copies = []

    def forward(which, source, rel, owner):
        for bit in bits:
            if rel == 0 or bit < lowest(rel):
                copy = remote(
                    source,
                    pairs[which][1].at[owner],
                    dp_send.at[which, rel | bit],
                    dp_recv.at[which, rel | bit],
                    "dp",
                    jnp.bitwise_xor(me, bit),
                )
                copy.start()
                copies.append(copy)

    def arrive(rel):
        owner = jnp.bitwise_xor(me, rel)
        for which in (1, 0):
            block = pairs[which][1].at[owner]
            sems = (dp_send.at[which, rel], dp_recv.at[which, rel])
            remote(block, block, *sems, "dp", jnp.bitwise_xor(me, lowest(rel))).wait_recv()
            forward(which, block, rel, owner)

    def hand(source, slot, bit):
        copy = remote(
            source,
            xo_ref.at[slot],
            mp_send.at[slot],
            mp_recv.at[slot],
            "mp",
            jnp.bitwise_xor(mp, bit),
        )
        copy.start()
        return copy

    for which in (1, 0):
        forward(which, pairs[which][0], 0, me)
    across = hand(x_ref, 2, 2)
    beside = hand(x_ref, 1, 1)
    wo_ref[me] = w_ref[...]
    go_ref[me] = g_ref[...]
    xo_ref[0] = x_ref[...]
    order = sorted(range(1, n), key=lambda rel: (bin(rel).count("1"), -rel))
    for rel in order:
        if rel % 2 == 0:
            arrive(rel)
    across.wait_recv()
    corner = hand(xo_ref.at[2], 3, 1)
    for rel in order:
        if rel % 2 == 1:
            arrive(rel)
    beside.wait_recv()
    corner.wait_recv()
    for copy in copies + [across, beside, corner]:
        copy.wait_send()


def sum_kernel(
    n,
    q_ref,
    o_ref,
    g_ref,
    p_ref,
    rq_ref,
    ro_ref,
    rg_ref,
    rp_ref,
    q_in,
    o_in,
    g_in,
    q_out,
    o_out,
    g_out,
    p_in,
    p_out,
    g_mp,
    dp_send,
    dp_recv,
    p_send,
    p_recv,
    g_send,
    g_recv,
):
    me, mp = (lax.axis_index("dp"), lax.axis_index("mp"))
    greet(n, me, mp)
    sets = (
        (g_ref, g_in, g_out, rg_ref),
        (o_ref, o_in, o_out, ro_ref),
        (q_ref, q_in, q_out, rq_ref),
    )
    copies = []
    pieces = p_ref.shape[1] // WIN

    def launch(which, source, rel):
        copy = remote(
            source,
            sets[which][1].at[rel],
            dp_send.at[which, rel],
            dp_recv.at[which, rel],
            "dp",
            jnp.bitwise_xor(me, lowest(rel)),
        )
        copy.start()
        copies.append(copy)

    def total(which, rel):
        value = sets[which][0][jnp.bitwise_xor(me, rel)].astype(F32)
        arrivals = sets[which][1]
        for bit in bits_of(n):
            if rel == 0 or bit < lowest(rel):
                slot = rel | bit
                block = arrivals.at[slot]
                sems = (dp_send.at[which, slot], dp_recv.at[which, slot])
                remote(block, block, *sems, "dp", jnp.bitwise_xor(me, bit)).wait_recv()
                value = value + arrivals[slot].astype(F32)
        return value

    def hand(source, kind, piece, bit):
        copy = remote(
            source,
            p_in.at[kind, piece],
            p_send.at[kind, piece],
            p_recv.at[kind, piece],
            "mp",
            jnp.bitwise_xor(mp, bit),
        )
        copy.start()
        copies.append(copy)
        return copy

    levels = [
        [rel for rel in range(n - 1, 0, -1) if lowest(rel) == bit] for bit in bits_of(n)
    ]
    first = [rel | 1 for level in levels[1:] for rel in level] + [1]
    rows = [pl.ds(piece * WIN, WIN) for piece in range(pieces)]
    corner = [hand(p_ref.at[3, rows[i]], 0, i, 1) for i in range(pieces)]
    for rel in first:
        for which in range(3):
            launch(which, sets[which][0].at[jnp.bitwise_xor(me, rel)], rel)
    beside = [hand(p_ref.at[1, rows[i]], 1, i, 1) for i in range(pieces)]
    across = []
    for i in range(pieces):
        corner[i].wait_recv()
        p_out[i] = (p_ref[2, rows[i], :].astype(F32) + p_in[0, i].astype(F32)).astype(BF16)
        across.append(hand(p_out.at[i], 2, i, 2))
    for level in levels[1:]:
        for rel in level:
            for which in range(3):
                staged = sets[which][2]
                staged[rel] = total(which, rel).astype(staged.dtype)
                launch(which, staged.at[rel], rel)
    rg_ref[...] = total(0, 0)
    for step, bit in enumerate((1, 2)):
        g_mp[2 * step] = rg_ref[...]
        copy = remote(
            g_mp.at[2 * step],
            g_mp.at[2 * step + 1],
            g_send.at[step],
            g_recv.at[step],
            "mp",
            jnp.bitwise_xor(mp, bit),
        )
        copy.start()
        copies.append(copy)
        copy.wait_recv()
        rg_ref[...] = rg_ref[...] + g_mp[2 * step + 1]
    for i in range(pieces):
        beside[i].wait_recv()
        across[i].wait_recv()
        rp_ref[rows[i], :] = (
            p_ref[0, rows[i], :].astype(F32) + p_in[1, i].astype(F32) + p_in[2, i].astype(F32)
        )
    ro_ref[...] = total(1, 0)
    rq_ref[...] = total(2, 0)
    for copy in copies:
        copy.wait_send()


def comm_params(collective_id):
    return pltpu.CompilerParams(
        collective_id=collective_id, has_side_effects=True, vmem_limit_bytes=40 * 2**20
    )


def gather_all(weight, gain, rows):
    n = lax.axis_size("dp")
    vmem = pl.BlockSpec(memory_space=pltpu.VMEM)
    return pl.pallas_call(
        functools.partial(gather_kernel, n),
        out_shape=(
            jax.ShapeDtypeStruct((n,) + weight.shape, BF16),
            jax.ShapeDtypeStruct((n,) + gain.shape, F32),
            jax.ShapeDtypeStruct((4,) + rows.shape, BF16),
        ),
        in_specs=[vmem] * 3,
        out_specs=(vmem,) * 3,
        scratch_shapes=[
            pltpu.SemaphoreType.DMA((2, n)),
            pltpu.SemaphoreType.DMA((2, n)),
            pltpu.SemaphoreType.DMA((4,)),
            pltpu.SemaphoreType.DMA((4,)),
        ],
        compiler_params=comm_params(0),
        name="gather_all",
    )(weight, gain, rows)


def sum_all(qkv, out, gain, products):
    n = lax.axis_size("dp")
    vmem = pl.BlockSpec(memory_space=pltpu.VMEM)
    pieces = products.shape[1] // WIN
    piece = (WIN, products.shape[2])
    return pl.pallas_call(
        functools.partial(sum_kernel, n),
        out_shape=tuple(
            jax.ShapeDtypeStruct(item.shape[1:], F32) for item in (qkv, out, gain, products)
        ),
        in_specs=[vmem] * 4,
        out_specs=(vmem,) * 4,
        scratch_shapes=[pltpu.VMEM(item.shape, item.dtype) for item in (qkv, out, gain)] * 2
        + [
            pltpu.VMEM((3, pieces) + piece, BF16),
            pltpu.VMEM((pieces,) + piece, BF16),
            pltpu.VMEM((4,) + gain.shape[1:], F32),
            pltpu.SemaphoreType.DMA((3, n)),
            pltpu.SemaphoreType.DMA((3, n)),
            pltpu.SemaphoreType.DMA((3, pieces)),
            pltpu.SemaphoreType.DMA((3, pieces)),
            pltpu.SemaphoreType.DMA((2,)),
            pltpu.SemaphoreType.DMA((2,)),
        ],
        compiler_params=comm_params(1),
        name="sum_all",
    )(qkv, out, gain, products)


def gather_columns(shard):
    parts = lax.all_gather(shard, "dp", axis=0)
    return jnp.transpose(parts, (1, 0, 2)).reshape(shard.shape[0], -1)


def scatter_rows(grad):
    return lax.psum_scatter(grad.astype(BF16), "dp", scatter_dimension=0, tiled=True).astype(F32)


def body(
    layer_input,
    row_seq,
    qkv_weight,
    out_weight,
    in_weight,
    down_weight,
    attn_gain,
    mlp_gain,
    cotangent,
):
    me = lax.axis_index("mp")
    me_arg = me.reshape(1).astype(jnp.int32)
    share, model = layer_input.shape
    width = qkv_weight.shape[2]
    units = in_weight.shape[2]
    own = attn_gain.shape[0]
    lanes = -(-own // 128) * 128
    gain_rows = jnp.pad(
        jnp.stack([attn_gain, mlp_gain]).astype(F32), ((0, 6), (0, lanes - own))
    )
    w_qkv, gains, x_all = gather_all(
        qkv_weight.reshape(-1, 3 * width), gain_rows, layer_input
    )
    w_qkv = w_qkv.reshape(model, 3 * width)
    gain_one, gain_two = (gains[:, row, :own].reshape(model) for row in range(2))
    w_out = gather_columns(out_weight)
    in_shard, w_out = lax.optimization_barrier((in_weight.reshape(-1, 2 * units), w_out))
    w_in = lax.all_gather(in_shard, "dp", axis=0, tiled=True)
    down_shard, w_in = lax.optimization_barrier((down_weight, w_in))
    w_gate, w_up = (w_in[:, :units], w_in[:, units:])
    w_down = gather_columns(down_shard)

    quarters = jnp.stack(spread(row_seq))
    seq_all = jnp.take(quarters, jnp.arange(4) ^ me, axis=0).reshape(-1)
    group_rows = seq_all.shape[0]
    blocks = group_rows // WIN
    cosine, sine = rotation_tables(positions(seq_all))
    padded_seq = jnp.pad(seq_all, (WIN // 2, WIN // 2), constant_values=-5).reshape(-1, WIN)
    seq_rows = jnp.concatenate([padded_seq[:-1], padded_seq[1:]], axis=1).reshape(
        blocks, 1, 2 * WIN
    )
    tables = (cosine, sine, seq_all[:, None], seq_rows)

    grad_final = cotangent.astype(F32) * (row_seq >= 0).astype(F32)[:, None]
    grad_parts = spread(grad_final.astype(BF16))

    block_in = layer_input.astype(F32)
    normed_one, factor_one = normalize(block_in)
    normed_all = normalize(x_all.reshape(-1, model).astype(F32))[0]
    h_all = (normed_all * gain_one).astype(BF16)
    qkv = [
        jnp.dot(
            h_all, w_qkv[:, part * width : (part + 1) * width], preferred_element_type=F32
        ).reshape(4, share, width)
        for part in range(3)
    ]
    mixed, queries, keys, values = attend_forward(me_arg, qkv, tables)
    grad_parts, mixed = lax.optimization_barrier((grad_parts, mixed))
    middle = block_in + collect(
        lambda r: jnp.dot(mixed[r], w_out, preferred_element_type=F32)
    )
    normed_two, factor_two = normalize(middle)
    h2_parts = spread((normed_two * gain_two).astype(BF16))

    def product(gate_in, up_in):
        return jax.nn.gelu(gate_in, approximate=False) * up_in

    halves = []
    for start in (0, 2):
        h_rows = jnp.concatenate(h2_parts[start : start + 2], axis=0)
        g_rows = jnp.concatenate(grad_parts[start : start + 2], axis=0)
        gate_vals = jnp.dot(h_rows, w_gate, preferred_element_type=F32)
        up_values = jnp.dot(h_rows, w_up, preferred_element_type=F32)
        value, pullback = jax.vjp(product, gate_vals, up_values)
        grad_gate, grad_up = pullback(dot_nt(g_rows, w_down))
        halves.append(
            (h_rows, g_rows, value.astype(BF16), grad_gate.astype(BF16), grad_up.astype(BF16))
        )

    def quarter_of(part, r):
        return halves[r // 2][part][(r % 2) * share : (r % 2 + 1) * share]

    grad_h_two = collect(
        lambda r: dot_nt(quarter_of(3, r), w_gate) + dot_nt(quarter_of(4, r), w_up)
    )
    h2_all, grad_all, hidden, grad_gate, grad_up = [
        jnp.concatenate(pair, axis=0) for pair in zip(*halves)
    ]
    down_share = scatter_rows(dot_tn(grad_all, hidden)).T
    in_share = scatter_rows(
        jnp.concatenate([dot_tn(h2_all, grad_gate), dot_tn(h2_all, grad_up)], axis=1)
    ).reshape(-1, 2, units)
    grad_norm_two, gain_two_grad = norm_back(grad_h_two, normed_two, factor_two, gain_two)
    grad_middle = grad_final + grad_norm_two
    grad_mid_own, late_hidden = lax.optimization_barrier(
        (grad_middle.astype(BF16), [item[2] for item in halves])
    )
    grad_mid_all = jnp.concatenate(spread(grad_mid_own), axis=0)
    activations = (
        middle
        + collect(
            lambda r: jnp.dot(
                late_hidden[r // 2][(r % 2) * share : (r % 2 + 1) * share],
                w_down,
                preferred_element_type=F32,
            )
        )
    ).astype(BF16)
    grad_mixed = dot_nt(grad_mid_all, w_out).astype(BF16).reshape(4, share, width)
    grad_qkv = attend_backward(me_arg, queries, keys, values, grad_mixed, tables)
    flat_grad = grad_qkv.reshape(group_rows, 3 * width)
    n = lax.axis_size("dp")
    products = dot_nt(flat_grad, w_qkv)
    gain_one_grad = jnp.sum(products * normed_all, axis=0)
    gain_grads = jnp.stack([gain_one_grad, gain_two_grad]).reshape(2, n, own)
    gain_grads = jnp.pad(jnp.transpose(gain_grads, (1, 0, 2)), ((0, 0), (0, 6), (0, lanes - own)))
    qkv_share, out_share, gain_total, grad_h_one = sum_all(
        dot_tn(h_all, flat_grad).astype(BF16).reshape(n, -1, 3 * width),
        dot_tn(grad_mid_all, mixed.reshape(group_rows, width)).astype(BF16).reshape(n, -1, width),
        gain_grads,
        products.astype(BF16).reshape(4, share, model),
    )
    grad_norm_one, _ = norm_back(grad_h_one, normed_one, factor_one, gain_one)
    input_grad = (grad_middle + grad_norm_one).astype(BF16)
    qkv_share = qkv_share.reshape(-1, 3, width)
    out_share = out_share.T
    gain_total = gain_total[:2, :own]
    return (
        activations,
        input_grad,
        gain_total[0],
        gain_total[1],
        qkv_share,
        out_share,
        in_share,
        down_share,
    )


def solution(mesh):
    in_specs = (
        P(("dp", "mp"), None),
        P(("dp", "mp")),
        P("dp", None, "mp"),
        P("mp", "dp"),
        P("dp", None, "mp"),
        P("mp", "dp"),
        P("dp"),
        P("dp"),
        P(("dp", "mp"), None),
    )
    out_specs = (
        P(("dp", "mp"), None),
        P(("dp", "mp"), None),
        P("dp"),
        P("dp"),
        P("dp", None, "mp"),
        P("mp", "dp"),
        P("dp", None, "mp"),
        P("mp", "dp"),
    )
    return jax.shard_map(body, mesh=mesh, in_specs=in_specs, out_specs=out_specs, check_vma=False)
```

```python
import functools
import math

import jax
import jax.numpy as jnp
import numpy as np
from jax import lax
from jax.experimental import pallas as pl
from jax.experimental.pallas import tpu as pltpu
from jax.sharding import PartitionSpec as P

HEAD_DIM = 64
WIN = 128
EPSILON = 1e-05
THETA_BASE = 10000.0
BF16 = jnp.bfloat16
MESH = pl.DeviceIdType.MESH
F32 = jnp.float32


def normalize(block_in):
    row_mean = jnp.mean(block_in, axis=-1, keepdims=True)
    centred = block_in - row_mean
    variance = jnp.mean(centred * centred, axis=-1, keepdims=True)
    factor = lax.rsqrt(variance + EPSILON)
    return (centred * factor, factor)


def norm_back(grad_in, normed, factor, gain):
    scaled = grad_in * gain
    centred_grad = (
        scaled
        - jnp.mean(scaled, axis=-1, keepdims=True)
        - normed * jnp.mean(scaled * normed, axis=-1, keepdims=True)
    )
    return (factor * centred_grad, jnp.sum(grad_in * normed, axis=0))


def positions(sequence):
    length = sequence.shape[0]
    row_index = jnp.arange(length, dtype=jnp.int32)
    before = jnp.concatenate([jnp.full((1,), -7, jnp.int32), sequence[:-1]])
    run_start = lax.cummax(jnp.where(sequence != before, row_index, 0), axis=0)
    return row_index - run_start


def rotation_tables(length):
    half = HEAD_DIM // 2
    frequency = np.exp(
        np.arange(half, dtype=np.float32) * np.float32(-2.0 * math.log(THETA_BASE) / HEAD_DIM)
    )
    angles = np.arange(length, dtype=np.float32)[:, None] * frequency[None, :]
    cosine, sine = (np.cos(angles), np.sin(angles))
    return (
        jnp.asarray(np.concatenate([cosine] * 4, axis=1)),
        jnp.asarray(np.concatenate([-sine, sine, -sine, sine], axis=1)),
    )


def turn(tensor, cosine, signed_sine):
    lane = lax.broadcasted_iota(jnp.int32, cosine.shape, 1)
    first = (lane % HEAD_DIM) < HEAD_DIM // 2
    parts = []
    for start in range(0, tensor.shape[1], 128):
        piece = tensor[:, start : start + 128]
        other = jnp.where(first, pltpu.roll(piece, 96, 1), pltpu.roll(piece, 32, 1))
        parts.append(piece * cosine + other * signed_sine)
    return jnp.concatenate(parts, axis=1)


def head_masks(heads, width):
    lane = lax.broadcasted_iota(jnp.int32, (WIN, width), 1)
    return [(lane // HEAD_DIM == head).astype(F32) for head in range(heads)]


def allowed_pairs(seq_col, seq_row):
    query = lax.broadcasted_iota(jnp.int32, (WIN, 2 * WIN), 0) + WIN // 2
    key = lax.broadcasted_iota(jnp.int32, (WIN, 2 * WIN), 1)
    distance = jnp.abs(query - key)
    same_run = (seq_col == seq_row) & (seq_col >= 0) & (distance <= WIN // 2)
    return same_run | (distance == 0)


def place_of(block, me, per_quarter):
    quarter = lax.div(block, per_quarter)
    start = pl.multiple_of(lax.rem(block, per_quarter) * WIN, WIN)
    return (jnp.bitwise_xor(quarter, me), pl.ds(start, WIN))


def probabilities_of(queries, keys, allowed, masks):
    heads = len(masks)
    stacked = jnp.concatenate([queries * mask.astype(BF16) for mask in masks], axis=0)
    scores = lax.dot_general(
        stacked, keys, (((1,), (1,)), ((), ())), preferred_element_type=F32
    ) * (1.0 / math.sqrt(HEAD_DIM))
    scores = scores.reshape(heads, WIN, 2 * WIN)
    scores = jnp.where(allowed[None], scores, -1e30)
    weights = jnp.exp(scores - jnp.max(scores, axis=-1, keepdims=True))
    total = jnp.sum(weights, axis=-1, keepdims=True)
    return (stacked, weights * (1.0 / total))


def forward_kernel(
    me_ref, base_ref, qi_ref, ki_ref, vi_ref, cos_ref, sin_ref, col_ref, row_ref, o_ref, q_ref, k_ref, v_ref
):
    me = me_ref[0]
    rows, width = q_ref.shape
    blocks = rows // WIN
    per_quarter = qi_ref.shape[1] // WIN
    half = WIN // 2
    for ref in (k_ref, v_ref):
        ref[0:half, :] = jnp.zeros((half, width), BF16)
        ref[rows + half : rows + 2 * half, :] = jnp.zeros((half, width), BF16)

    def turn_block(block, carry):
        quarter, inner = place_of(block, me, per_quarter)
        start = pl.multiple_of(block * WIN, WIN)
        here = pl.ds(start, WIN)
        later = pl.ds(pl.multiple_of(start + half, half), WIN)
        place = pl.ds(pl.multiple_of(base_ref[block] * WIN, WIN), WIN)
        cosine, sine = (cos_ref[place, :], sin_ref[place, :])
        q_ref[here, :] = turn(qi_ref[quarter, inner, :], cosine, sine).astype(BF16)
        k_ref[later, :] = turn(ki_ref[quarter, inner, :], cosine, sine).astype(BF16)
        v_ref[later, :] = vi_ref[quarter, inner, :].astype(BF16)
        return carry

    lax.fori_loop(0, blocks, turn_block, 0)
    masks = head_masks(width // HEAD_DIM, width)

    def attend_block(block, carry):
        quarter, inner = place_of(block, me, per_quarter)
        start = pl.multiple_of(block * WIN, WIN)
        span = pl.ds(start, 2 * WIN)
        allowed = allowed_pairs(col_ref[pl.ds(start, WIN), :], row_ref[block])
        _, prob = probabilities_of(q_ref[pl.ds(start, WIN), :], k_ref[span, :], allowed, masks)
        prob = prob.astype(BF16).reshape(-1, 2 * WIN)
        mixed = jnp.dot(prob, v_ref[span, :], preferred_element_type=F32)
        mixed = mixed.reshape(len(masks), WIN, width)
        o_ref[quarter, inner, :] = sum(
            mixed[head] * mask for head, mask in enumerate(masks)
        ).astype(BF16)
        return carry

    lax.fori_loop(0, blocks, attend_block, 0)


def backward_kernel(
    me_ref, base_ref, q_ref, k_ref, v_ref, g_ref, cos_ref, sin_ref, col_ref, row_ref, d_ref, dk_ref, dv_ref
):
    me = me_ref[0]
    rows, width = q_ref.shape
    blocks = rows // WIN
    per_quarter = g_ref.shape[1] // WIN
    half = WIN // 2
    factor = 1.0 / math.sqrt(HEAD_DIM)
    dk_ref[...] = jnp.zeros(dk_ref.shape, F32)
    dv_ref[...] = jnp.zeros(dv_ref.shape, F32)
    masks = head_masks(width // HEAD_DIM, width)
    over_rows = (((0,), (0,)), ((), ()))

    def attend_block(block, carry):
        quarter, inner = place_of(block, me, per_quarter)
        start = pl.multiple_of(block * WIN, WIN)
        here = pl.ds(start, WIN)
        span = pl.ds(start, 2 * WIN)
        allowed = allowed_pairs(col_ref[here, :], row_ref[block])
        keys = k_ref[span, :]
        place = pl.ds(pl.multiple_of(base_ref[block] * WIN, WIN), WIN)
        queries, prob = probabilities_of(q_ref[here, :], keys, allowed, masks)
        grads = g_ref[quarter, inner, :]
        grads = jnp.concatenate([grads * mask.astype(BF16) for mask in masks], axis=0)
        grad_prob = lax.dot_general(
            grads, v_ref[span, :], (((1,), (1,)), ((), ())), preferred_element_type=F32
        ).reshape(prob.shape)
        inner_sum = jnp.sum(prob * grad_prob, axis=-1, keepdims=True)
        grad_score = (prob * (grad_prob - inner_sum)).astype(BF16).reshape(-1, 2 * WIN)
        prob = prob.astype(BF16).reshape(-1, 2 * WIN)
        dv_ref[span, :] += lax.dot_general(prob, grads, over_rows, preferred_element_type=F32)
        dk_ref[span, :] += lax.dot_general(
            grad_score, queries, over_rows, preferred_element_type=F32
        )
        grad_query = jnp.dot(grad_score, keys, preferred_element_type=F32)
        grad_query = grad_query.reshape(len(masks), WIN, width)
        grad_query = sum(grad_query[head] * mask for head, mask in enumerate(masks)) * factor
        d_ref[quarter, inner, 0:width] = turn(
            grad_query, cos_ref[place, :], -sin_ref[place, :]
        ).astype(BF16)
        return carry

    lax.fori_loop(0, blocks, attend_block, 0)

    def finish_block(block, carry):
        quarter, inner = place_of(block, me, per_quarter)
        start = pl.multiple_of(block * WIN, WIN)
        place = pl.ds(pl.multiple_of(base_ref[block] * WIN, WIN), WIN)
        later = pl.ds(pl.multiple_of(start + half, half), WIN)
        d_ref[quarter, inner, width : 2 * width] = turn(
            dk_ref[later, :] * factor, cos_ref[place, :], -sin_ref[place, :]
        ).astype(BF16)
        d_ref[quarter, inner, 2 * width : 3 * width] = dv_ref[later, :].astype(BF16)
        return carry

    lax.fori_loop(0, blocks, finish_block, 0)


def vmem_specs(count):
    return [pl.BlockSpec(memory_space=pltpu.SMEM)] * 2 + [pl.BlockSpec(memory_space=pltpu.VMEM)] * count


def attend_forward(me, base, qkv, tables):
    quarters, share, width = qkv[0].shape
    rows = quarters * share
    padded = jax.ShapeDtypeStruct((rows + WIN, width), BF16)
    return pl.pallas_call(
        forward_kernel,
        out_shape=(
            jax.ShapeDtypeStruct((quarters, share, width), BF16),
            jax.ShapeDtypeStruct((rows, width), BF16),
            padded,
            padded,
        ),
        in_specs=vmem_specs(7),
        out_specs=(pl.BlockSpec(memory_space=pltpu.VMEM),) * 4,
        compiler_params=pltpu.CompilerParams(vmem_limit_bytes=40 * 2**20),
        cost_estimate=pl.CostEstimate(
            flops=16 * rows * WIN * width, bytes_accessed=16 * rows * width, transcendentals=0
        ),
        name="attend_forward",
    )(me, base, *qkv, *tables)


def attend_backward(me, base, queries, keys, values, grads, tables):
    quarters, share, width = grads.shape
    rows = quarters * share
    accumulator = pltpu.VMEM((rows + WIN, width), F32)
    return pl.pallas_call(
        backward_kernel,
        out_shape=jax.ShapeDtypeStruct((quarters, share, 3 * width), BF16),
        in_specs=vmem_specs(8),
        out_specs=pl.BlockSpec(memory_space=pltpu.VMEM),
        scratch_shapes=[accumulator, accumulator],
        compiler_params=pltpu.CompilerParams(vmem_limit_bytes=40 * 2**20),
        cost_estimate=pl.CostEstimate(
            flops=40 * rows * WIN * width, bytes_accessed=16 * rows * width, transcendentals=0
        ),
        name="attend_backward",
    )(me, base, queries, keys, values, grads, *tables)


def swap(tensor, bit):
    return lax.ppermute(tensor, "mp", [(i, i ^ bit) for i in range(4)])


def spread(rows):
    across = swap(rows, 2)
    return [rows, swap(rows, 1), across, swap(across, 1)]


def collect(product):
    away = [swap(product(r).astype(BF16), 1) for r in (3, 1)]
    across = swap((product(2) + away[0].astype(F32)).astype(BF16), 2)
    return product(0) + away[1].astype(F32) + across.astype(F32)


def dot_nt(left, right):
    return lax.dot_general(left, right, (((1,), (1,)), ((), ())), preferred_element_type=F32)


def dot_tn(left, right):
    return lax.dot_general(left, right, (((0,), (0,)), ((), ())), preferred_element_type=F32)


def bits_of(count):
    return [2**place for place in range(count.bit_length() - 1)]


def lowest(value):
    return value & -value


def greet(n, me, mp):
    barrier = pltpu.get_barrier_semaphore()
    partners = [{"dp": jnp.bitwise_xor(me, bit)} for bit in bits_of(n)]
    partners += [{"mp": jnp.bitwise_xor(mp, bit)} for bit in (1, 2)]
    for partner in partners:
        pl.semaphore_signal(barrier, inc=1, device_id=partner, device_id_type=MESH)
    pl.semaphore_wait(barrier, len(partners))


def remote(source, target, send_sem, recv_sem, axis, device):
    return pltpu.make_async_remote_copy(
        src_ref=source,
        dst_ref=target,
        send_sem=send_sem,
        recv_sem=recv_sem,
        device_id={axis: device},
        device_id_type=MESH,
    )


def gather_kernel(
    n, w_ref, g_ref, x_ref, s_ref, wo_ref, go_ref, xo_ref, so_ref, dp_send, dp_recv, mp_send, mp_recv
):
    me, mp = (lax.axis_index("dp"), lax.axis_index("mp"))
    greet(n, me, mp)
    pairs = ((w_ref, wo_ref), (g_ref, go_ref))
    bits = bits_of(n)[::-1]
    copies = []

    def forward(which, source, rel, owner):
        for bit in bits:
            if rel == 0 or bit < lowest(rel):
                copy = remote(
                    source,
                    pairs[which][1].at[owner],
                    dp_send.at[which, rel | bit],
                    dp_recv.at[which, rel | bit],
                    "dp",
                    jnp.bitwise_xor(me, bit),
                )
                copy.start()
                copies.append(copy)

    def arrive(rel):
        owner = jnp.bitwise_xor(me, rel)
        for which in (1, 0):
            block = pairs[which][1].at[owner]
            sems = (dp_send.at[which, rel], dp_recv.at[which, rel])
            remote(block, block, *sems, "dp", jnp.bitwise_xor(me, lowest(rel))).wait_recv()
            forward(which, block, rel, owner)

    def hand(which, source, slot, bit):
        copy = remote(
            source,
            (xo_ref, so_ref)[which].at[slot],
            mp_send.at[which, slot],
            mp_recv.at[which, slot],
            "mp",
            jnp.bitwise_xor(mp, bit),
        )
        copy.start()
        return copy

    for which in (1, 0):
        forward(which, pairs[which][0], 0, me)
    across = [hand(1, s_ref, 2, 2), hand(0, x_ref, 2, 2)]
    beside = [hand(1, s_ref, 1, 1), hand(0, x_ref, 1, 1)]
    wo_ref[me] = w_ref[...]
    go_ref[me] = g_ref[...]
    xo_ref[0] = x_ref[...]
    so_ref[0] = s_ref[...]
    order = sorted(range(1, n), key=lambda rel: (bin(rel).count("1"), -rel))
    for rel in order:
        if rel % 2 == 0:
            arrive(rel)
    corner = []
    for which, target in ((1, so_ref), (0, xo_ref)):
        across[1 - which].wait_recv()
        corner.append(hand(which, target.at[2], 3, 1))
    for rel in order:
        if rel % 2 == 1:
            arrive(rel)
    for copy in beside + corner:
        copy.wait_recv()
    for copy in copies + across + beside + corner:
        copy.wait_send()


def sum_kernel(
    n,
    q_ref,
    o_ref,
    g_ref,
    p_ref,
    rq_ref,
    ro_ref,
    rg_ref,
    rp_ref,
    q_in,
    o_in,
    g_in,
    q_out,
    o_out,
    g_out,
    p_in,
    p_out,
    g_mp,
    dp_send,
    dp_recv,
    p_send,
    p_recv,
    g_send,
    g_recv,
):
    me, mp = (lax.axis_index("dp"), lax.axis_index("mp"))
    greet(n, me, mp)
    sets = (
        (g_ref, g_in, g_out, rg_ref),
        (o_ref, o_in, o_out, ro_ref),
        (q_ref, q_in, q_out, rq_ref),
    )
    copies = []
    pieces = p_ref.shape[1] // WIN

    def launch(which, source, rel):
        copy = remote(
            source,
            sets[which][1].at[rel],
            dp_send.at[which, rel],
            dp_recv.at[which, rel],
            "dp",
            jnp.bitwise_xor(me, lowest(rel)),
        )
        copy.start()
        copies.append(copy)

    def total(which, rel):
        value = sets[which][0][jnp.bitwise_xor(me, rel)].astype(F32)
        arrivals = sets[which][1]
        for bit in bits_of(n):
            if rel == 0 or bit < lowest(rel):
                slot = rel | bit
                block = arrivals.at[slot]
                sems = (dp_send.at[which, slot], dp_recv.at[which, slot])
                remote(block, block, *sems, "dp", jnp.bitwise_xor(me, bit)).wait_recv()
                value = value + arrivals[slot].astype(F32)
        return value

    def hand(source, kind, piece, bit):
        copy = remote(
            source,
            p_in.at[kind, piece],
            p_send.at[kind, piece],
            p_recv.at[kind, piece],
            "mp",
            jnp.bitwise_xor(mp, bit),
        )
        copy.start()
        copies.append(copy)
        return copy

    levels = [
        [rel for rel in range(n - 1, 0, -1) if lowest(rel) == bit] for bit in bits_of(n)
    ]
    first = [rel | 1 for level in levels[1:] for rel in level] + [1]
    rows = [pl.ds(piece * WIN, WIN) for piece in range(pieces)]
    corner = [hand(p_ref.at[3, rows[i]], 0, i, 1) for i in range(pieces)]
    for rel in first:
        for which in range(3):
            launch(which, sets[which][0].at[jnp.bitwise_xor(me, rel)], rel)
    beside = [hand(p_ref.at[1, rows[i]], 1, i, 1) for i in range(pieces)]
    across = []
    for i in range(pieces):
        corner[i].wait_recv()
        p_out[i] = (p_ref[2, rows[i], :].astype(F32) + p_in[0, i].astype(F32)).astype(BF16)
        across.append(hand(p_out.at[i], 2, i, 2))
    for level in levels[1:]:
        for rel in level:
            for which in range(3):
                staged = sets[which][2]
                staged[rel] = total(which, rel).astype(staged.dtype)
                launch(which, staged.at[rel], rel)
    rg_ref[...] = total(0, 0)
    for step, bit in enumerate((1, 2)):
        g_mp[2 * step] = rg_ref[...]
        copy = remote(
            g_mp.at[2 * step],
            g_mp.at[2 * step + 1],
            g_send.at[step],
            g_recv.at[step],
            "mp",
            jnp.bitwise_xor(mp, bit),
        )
        copy.start()
        copies.append(copy)
        copy.wait_recv()
        rg_ref[...] = rg_ref[...] + g_mp[2 * step + 1]
    for i in range(pieces):
        beside[i].wait_recv()
        across[i].wait_recv()
        rp_ref[rows[i], :] = (
            p_ref[0, rows[i], :].astype(F32) + p_in[1, i].astype(F32) + p_in[2, i].astype(F32)
        )
    ro_ref[...] = total(1, 0)
    rq_ref[...] = total(2, 0)
    for copy in copies:
        copy.wait_send()


def comm_params(collective_id):
    return pltpu.CompilerParams(
        collective_id=collective_id, has_side_effects=True, vmem_limit_bytes=40 * 2**20
    )


def gather_all(weight, gain, rows, sequence):
    n = lax.axis_size("dp")
    vmem = pl.BlockSpec(memory_space=pltpu.VMEM)
    return pl.pallas_call(
        functools.partial(gather_kernel, n),
        out_shape=(
            jax.ShapeDtypeStruct((n,) + weight.shape, BF16),
            jax.ShapeDtypeStruct((n,) + gain.shape, F32),
            jax.ShapeDtypeStruct((4,) + rows.shape, BF16),
            jax.ShapeDtypeStruct((4,) + sequence.shape, jnp.int32),
        ),
        in_specs=[vmem] * 4,
        out_specs=(vmem,) * 4,
        scratch_shapes=[
            pltpu.SemaphoreType.DMA((2, n)),
            pltpu.SemaphoreType.DMA((2, n)),
            pltpu.SemaphoreType.DMA((2, 4)),
            pltpu.SemaphoreType.DMA((2, 4)),
        ],
        compiler_params=comm_params(0),
        name="gather_all",
    )(weight, gain, rows, sequence)


def sum_all(qkv, out, gain, products):
    n = lax.axis_size("dp")
    vmem = pl.BlockSpec(memory_space=pltpu.VMEM)
    pieces = products.shape[1] // WIN
    piece = (WIN, products.shape[2])
    return pl.pallas_call(
        functools.partial(sum_kernel, n),
        out_shape=tuple(
            jax.ShapeDtypeStruct(item.shape[1:], F32) for item in (qkv, out, gain, products)
        ),
        in_specs=[vmem] * 4,
        out_specs=(vmem,) * 4,
        scratch_shapes=[pltpu.VMEM(item.shape, item.dtype) for item in (qkv, out, gain)] * 2
        + [
            pltpu.VMEM((3, pieces) + piece, BF16),
            pltpu.VMEM((pieces,) + piece, BF16),
            pltpu.VMEM((4,) + gain.shape[1:], F32),
            pltpu.SemaphoreType.DMA((3, n)),
            pltpu.SemaphoreType.DMA((3, n)),
            pltpu.SemaphoreType.DMA((3, pieces)),
            pltpu.SemaphoreType.DMA((3, pieces)),
            pltpu.SemaphoreType.DMA((2,)),
            pltpu.SemaphoreType.DMA((2,)),
        ],
        compiler_params=comm_params(1),
        name="sum_all",
    )(qkv, out, gain, products)


def gather_columns(shard):
    parts = lax.all_gather(shard, "dp", axis=0)
    return jnp.transpose(parts, (1, 0, 2)).reshape(shard.shape[0], -1)


def scatter_rows(grad):
    return lax.psum_scatter(grad.astype(BF16), "dp", scatter_dimension=0, tiled=True).astype(F32)


def body(
    layer_input,
    row_seq,
    qkv_weight,
    out_weight,
    in_weight,
    down_weight,
    attn_gain,
    mlp_gain,
    cotangent,
):
    me = lax.axis_index("mp")
    me_arg = me.reshape(1).astype(jnp.int32)
    share, model = layer_input.shape
    width = qkv_weight.shape[2]
    units = in_weight.shape[2]
    own = attn_gain.shape[0]
    lanes = -(-own // 128) * 128
    gain_rows = jnp.pad(
        jnp.stack([attn_gain, mlp_gain]).astype(F32), ((0, 6), (0, lanes - own))
    )
    tiles = share // WIN
    first_shard = jnp.concatenate([qkv_weight.reshape(-1, 3 * width), out_weight.T], axis=1)
    first, gains, x_all, quarters = gather_all(
        first_shard,
        gain_rows,
        layer_input,
        jnp.pad(row_seq.reshape(tiles, WIN), ((0, -tiles % 8), (0, 0))),
    )
    first = first.reshape(model, 4 * width)
    w_qkv, w_out = (first[:, : 3 * width], first[:, 3 * width :])
    gain_one, gain_two = (gains[:, row, :own].reshape(model) for row in range(2))
    w_gate, w_up, w_down = [
        lax.all_gather(item, "dp", axis=0, tiled=True)
        for item in (in_weight[:, 0], in_weight[:, 1], down_weight.T)
    ]

    seq_all = jnp.take(quarters[:, :tiles], jnp.arange(4) ^ me, axis=0).reshape(-1)
    group_rows = seq_all.shape[0]
    blocks = group_rows // WIN
    base = positions(seq_all.reshape(blocks, WIN)[:, 0])
    padded_seq = jnp.pad(seq_all, (WIN // 2, WIN // 2), constant_values=-5).reshape(-1, WIN)
    seq_rows = jnp.concatenate([padded_seq[:-1], padded_seq[1:]], axis=1).reshape(
        blocks, 1, 2 * WIN
    )
    tables = (*rotation_tables(group_rows), seq_all[:, None], seq_rows)

    grad_final = cotangent.astype(F32) * (row_seq >= 0).astype(F32)[:, None]
    grad_parts = spread(grad_final.astype(BF16))

    block_in = layer_input.astype(F32)
    normed_one, factor_one = normalize(block_in)
    normed_all = normalize(x_all.reshape(-1, model).astype(F32))[0]
    h_all = (normed_all * gain_one).astype(BF16)
    qkv = [
        jnp.dot(
            h_all, w_qkv[:, part * width : (part + 1) * width], preferred_element_type=F32
        ).reshape(4, share, width)
        for part in range(3)
    ]
    mixed, queries, keys, values = attend_forward(me_arg, base, qkv, tables)
    grad_parts, mixed = lax.optimization_barrier((grad_parts, mixed))
    middle = block_in + collect(
        lambda r: dot_nt(mixed[r], w_out)
    )
    normed_two, factor_two = normalize(middle)
    h2_own = (normed_two * gain_two).astype(BF16)
    h2_across = swap(h2_own, 2)
    h2_parts = [h2_own, swap(h2_own, 1)]

    def product(gate_in, up_in):
        return jax.nn.gelu(gate_in, approximate=False) * up_in

    halves = []
    for start in (0, 2):
        if start:
            h2_across, halves[0] = lax.optimization_barrier((h2_across, halves[0]))
            h2_parts += [h2_across, swap(h2_across, 1)]
        h_rows = jnp.concatenate(h2_parts[start : start + 2], axis=0)
        g_rows = jnp.concatenate(grad_parts[start : start + 2], axis=0)
        gate_vals = jnp.dot(h_rows, w_gate, preferred_element_type=F32)
        up_values = jnp.dot(h_rows, w_up, preferred_element_type=F32)
        value, pullback = jax.vjp(product, gate_vals, up_values)
        grad_gate, grad_up = pullback(jnp.dot(g_rows, w_down, preferred_element_type=F32))
        halves.append(
            (h_rows, g_rows, value.astype(BF16), grad_gate.astype(BF16), grad_up.astype(BF16))
        )

    def quarter_of(part, r):
        return halves[r // 2][part][(r % 2) * share : (r % 2 + 1) * share]

    grad_h_two = collect(
        lambda r: dot_nt(quarter_of(3, r), w_gate) + dot_nt(quarter_of(4, r), w_up)
    )
    h2_all, grad_all, hidden, grad_gate, grad_up = [
        jnp.concatenate(pair, axis=0) for pair in zip(*halves)
    ]
    down_share = scatter_rows(dot_tn(grad_all, hidden)).T
    in_partial = jnp.concatenate(
        [dot_tn(h2_all, grad_gate).astype(BF16), dot_tn(h2_all, grad_up).astype(BF16)], axis=1
    )
    grad_norm_two, gain_two_grad = norm_back(grad_h_two, normed_two, factor_two, gain_two)
    grad_middle = grad_final + grad_norm_two
    grad_mid_own, in_partial, late_hidden = lax.optimization_barrier(
        (grad_middle.astype(BF16), in_partial, [item[2] for item in halves])
    )
    in_share = scatter_rows(in_partial).reshape(-1, 2, units)
    grad_mid_all = jnp.concatenate(spread(grad_mid_own), axis=0)
    activations = (
        middle
        + collect(
            lambda r: dot_nt(
                late_hidden[r // 2][(r % 2) * share : (r % 2 + 1) * share], w_down
            )
        )
    ).astype(BF16)
    grad_mixed = jnp.dot(grad_mid_all, w_out, preferred_element_type=F32).astype(BF16).reshape(4, share, width)
    grad_qkv = attend_backward(me_arg, base, queries, keys, values, grad_mixed, tables)
    flat_grad = grad_qkv.reshape(group_rows, 3 * width)
    n = lax.axis_size("dp")
    products = dot_nt(flat_grad, w_qkv)
    gain_one_grad = jnp.sum(products * normed_all, axis=0)
    gain_grads = jnp.stack([gain_one_grad, gain_two_grad]).reshape(2, n, own)
    gain_grads = jnp.pad(jnp.transpose(gain_grads, (1, 0, 2)), ((0, 0), (0, 6), (0, lanes - own)))
    qkv_share, out_share, gain_total, grad_h_one = sum_all(
        dot_tn(h_all, flat_grad).astype(BF16).reshape(n, -1, 3 * width),
        dot_tn(grad_mid_all, mixed.reshape(group_rows, width)).astype(BF16).reshape(n, -1, width),
        gain_grads,
        products.astype(BF16).reshape(4, share, model),
    )
    grad_norm_one, _ = norm_back(grad_h_one, normed_one, factor_one, gain_one)
    input_grad = (grad_middle + grad_norm_one).astype(BF16)
    qkv_share = qkv_share.reshape(-1, 3, width)
    out_share = out_share.T
    gain_total = gain_total[:2, :own]
    return (
        activations,
        input_grad,
        gain_total[0],
        gain_total[1],
        qkv_share,
        out_share,
        in_share,
        down_share,
    )


def solution(mesh):
    in_specs = (
        P(("dp", "mp"), None),
        P(("dp", "mp")),
        P("dp", None, "mp"),
        P("mp", "dp"),
        P("dp", None, "mp"),
        P("mp", "dp"),
        P("dp"),
        P("dp"),
        P(("dp", "mp"), None),
    )
    out_specs = (
        P(("dp", "mp"), None),
        P(("dp", "mp"), None),
        P("dp"),
        P("dp"),
        P("dp", None, "mp"),
        P("mp", "dp"),
        P("dp", None, "mp"),
        P("mp", "dp"),
    )
    return jax.shard_map(body, mesh=mesh, in_specs=in_specs, out_specs=out_specs, check_vma=False)
```

```python
import functools
import math

import jax
import jax.numpy as jnp
import numpy as np
from jax import lax
from jax.experimental import pallas as pl
from jax.experimental.pallas import tpu as pltpu
from jax.sharding import PartitionSpec as P

HEAD_DIM = 64
WIN = 128
EPSILON = 1e-05
THETA_BASE = 10000.0
BF16 = jnp.bfloat16
MESH = pl.DeviceIdType.MESH
F32 = jnp.float32


def normalize(block_in):
    row_mean = jnp.mean(block_in, axis=-1, keepdims=True)
    centred = block_in - row_mean
    variance = jnp.mean(centred * centred, axis=-1, keepdims=True)
    factor = lax.rsqrt(variance + EPSILON)
    return (centred * factor, factor)


def norm_back(grad_in, normed, factor, gain):
    scaled = grad_in * gain
    centred_grad = (
        scaled
        - jnp.mean(scaled, axis=-1, keepdims=True)
        - normed * jnp.mean(scaled * normed, axis=-1, keepdims=True)
    )
    return (factor * centred_grad, jnp.sum(grad_in * normed, axis=0))


def positions(sequence):
    length = sequence.shape[0]
    row_index = jnp.arange(length, dtype=jnp.int32)
    before = jnp.concatenate([jnp.full((1,), -7, jnp.int32), sequence[:-1]])
    run_start = lax.cummax(jnp.where(sequence != before, row_index, 0), axis=0)
    return row_index - run_start


def rotation_tables(length):
    half = HEAD_DIM // 2
    frequency = np.exp(
        np.arange(half, dtype=np.float32) * np.float32(-2.0 * math.log(THETA_BASE) / HEAD_DIM)
    )
    angles = np.arange(length, dtype=np.float32)[:, None] * frequency[None, :]
    cosine, sine = (np.cos(angles), np.sin(angles))
    return (
        jnp.asarray(np.concatenate([cosine] * 4, axis=1)),
        jnp.asarray(np.concatenate([-sine, sine, -sine, sine], axis=1)),
    )


def turn(tensor, cosine, signed_sine):
    lane = lax.broadcasted_iota(jnp.int32, cosine.shape, 1)
    first = (lane % HEAD_DIM) < HEAD_DIM // 2
    parts = []
    for start in range(0, tensor.shape[1], 128):
        piece = tensor[:, start : start + 128]
        other = jnp.where(first, pltpu.roll(piece, 96, 1), pltpu.roll(piece, 32, 1))
        parts.append(piece * cosine + other * signed_sine)
    return jnp.concatenate(parts, axis=1)


def head_masks(heads, width):
    lane = lax.broadcasted_iota(jnp.int32, (WIN, width), 1)
    return [(lane // HEAD_DIM == head).astype(F32) for head in range(heads)]


def allowed_pairs(seq_col, seq_row):
    query = lax.broadcasted_iota(jnp.int32, (WIN, 2 * WIN), 0) + WIN // 2
    key = lax.broadcasted_iota(jnp.int32, (WIN, 2 * WIN), 1)
    distance = jnp.abs(query - key)
    same_run = (seq_col == seq_row) & (seq_col >= 0) & (distance <= WIN // 2)
    return same_run | (distance == 0)


def place_of(block, me, per_quarter):
    quarter = lax.div(block, per_quarter)
    start = pl.multiple_of(lax.rem(block, per_quarter) * WIN, WIN)
    return (jnp.bitwise_xor(quarter, me), pl.ds(start, WIN))


def probabilities_of(queries, keys, allowed, masks):
    heads = len(masks)
    stacked = jnp.concatenate([queries * mask.astype(BF16) for mask in masks], axis=0)
    scores = lax.dot_general(
        stacked, keys, (((1,), (1,)), ((), ())), preferred_element_type=F32
    ) * (1.0 / math.sqrt(HEAD_DIM))
    scores = scores.reshape(heads, WIN, 2 * WIN)
    scores = jnp.where(allowed[None], scores, -1e30)
    weights = jnp.exp(scores - jnp.max(scores, axis=-1, keepdims=True))
    total = jnp.sum(weights, axis=-1, keepdims=True)
    return (stacked, weights * (1.0 / total))


def forward_kernel(
    me_ref, base_ref, qi_ref, ki_ref, vi_ref, cos_ref, sin_ref, col_ref, row_ref, o_ref, q_ref, k_ref, v_ref
):
    me = me_ref[0]
    rows, width = q_ref.shape
    blocks = rows // WIN
    per_quarter = qi_ref.shape[1] // WIN
    half = WIN // 2
    for ref in (k_ref, v_ref):
        ref[0:half, :] = jnp.zeros((half, width), BF16)
        ref[rows + half : rows + 2 * half, :] = jnp.zeros((half, width), BF16)

    def turn_block(block, carry):
        quarter, inner = place_of(block, me, per_quarter)
        start = pl.multiple_of(block * WIN, WIN)
        here = pl.ds(start, WIN)
        later = pl.ds(pl.multiple_of(start + half, half), WIN)
        place = pl.ds(pl.multiple_of(base_ref[block] * WIN, WIN), WIN)
        cosine, sine = (cos_ref[place, :], sin_ref[place, :])
        q_ref[here, :] = turn(qi_ref[quarter, inner, :], cosine, sine).astype(BF16)
        k_ref[later, :] = turn(ki_ref[quarter, inner, :], cosine, sine).astype(BF16)
        v_ref[later, :] = vi_ref[quarter, inner, :].astype(BF16)
        return carry

    lax.fori_loop(0, blocks, turn_block, 0)
    masks = head_masks(width // HEAD_DIM, width)

    def attend_block(block, carry):
        quarter, inner = place_of(block, me, per_quarter)
        start = pl.multiple_of(block * WIN, WIN)
        span = pl.ds(start, 2 * WIN)
        allowed = allowed_pairs(col_ref[pl.ds(start, WIN), :], row_ref[block])
        _, prob = probabilities_of(q_ref[pl.ds(start, WIN), :], k_ref[span, :], allowed, masks)
        prob = prob.astype(BF16).reshape(-1, 2 * WIN)
        mixed = jnp.dot(prob, v_ref[span, :], preferred_element_type=F32)
        mixed = mixed.reshape(len(masks), WIN, width)
        o_ref[quarter, inner, :] = sum(
            mixed[head] * mask for head, mask in enumerate(masks)
        ).astype(BF16)
        return carry

    lax.fori_loop(0, blocks, attend_block, 0)


def backward_kernel(
    me_ref, base_ref, q_ref, k_ref, v_ref, g_ref, cos_ref, sin_ref, col_ref, row_ref, d_ref, dk_ref, dv_ref
):
    me = me_ref[0]
    rows, width = q_ref.shape
    blocks = rows // WIN
    per_quarter = g_ref.shape[1] // WIN
    half = WIN // 2
    factor = 1.0 / math.sqrt(HEAD_DIM)
    dk_ref[...] = jnp.zeros(dk_ref.shape, F32)
    dv_ref[...] = jnp.zeros(dv_ref.shape, F32)
    masks = head_masks(width // HEAD_DIM, width)
    over_rows = (((0,), (0,)), ((), ()))

    def attend_block(block, carry):
        quarter, inner = place_of(block, me, per_quarter)
        start = pl.multiple_of(block * WIN, WIN)
        here = pl.ds(start, WIN)
        span = pl.ds(start, 2 * WIN)
        allowed = allowed_pairs(col_ref[here, :], row_ref[block])
        keys = k_ref[span, :]
        place = pl.ds(pl.multiple_of(base_ref[block] * WIN, WIN), WIN)
        queries, prob = probabilities_of(q_ref[here, :], keys, allowed, masks)
        grads = g_ref[quarter, inner, :]
        grads = jnp.concatenate([grads * mask.astype(BF16) for mask in masks], axis=0)
        grad_prob = lax.dot_general(
            grads, v_ref[span, :], (((1,), (1,)), ((), ())), preferred_element_type=F32
        ).reshape(prob.shape)
        inner_sum = jnp.sum(prob * grad_prob, axis=-1, keepdims=True)
        grad_score = (prob * (grad_prob - inner_sum)).astype(BF16).reshape(-1, 2 * WIN)
        prob = prob.astype(BF16).reshape(-1, 2 * WIN)
        dv_ref[span, :] += lax.dot_general(prob, grads, over_rows, preferred_element_type=F32)
        dk_ref[span, :] += lax.dot_general(
            grad_score, queries, over_rows, preferred_element_type=F32
        )
        grad_query = jnp.dot(grad_score, keys, preferred_element_type=F32)
        grad_query = grad_query.reshape(len(masks), WIN, width)
        grad_query = sum(grad_query[head] * mask for head, mask in enumerate(masks)) * factor
        d_ref[quarter, inner, 0:width] = turn(
            grad_query, cos_ref[place, :], -sin_ref[place, :]
        ).astype(BF16)
        return carry

    lax.fori_loop(0, blocks, attend_block, 0)

    def finish_block(block, carry):
        quarter, inner = place_of(block, me, per_quarter)
        start = pl.multiple_of(block * WIN, WIN)
        place = pl.ds(pl.multiple_of(base_ref[block] * WIN, WIN), WIN)
        later = pl.ds(pl.multiple_of(start + half, half), WIN)
        d_ref[quarter, inner, width : 2 * width] = turn(
            dk_ref[later, :] * factor, cos_ref[place, :], -sin_ref[place, :]
        ).astype(BF16)
        d_ref[quarter, inner, 2 * width : 3 * width] = dv_ref[later, :].astype(BF16)
        return carry

    lax.fori_loop(0, blocks, finish_block, 0)


def vmem_specs(count):
    return [pl.BlockSpec(memory_space=pltpu.SMEM)] * 2 + [pl.BlockSpec(memory_space=pltpu.VMEM)] * count


def attend_forward(me, base, qkv, tables):
    quarters, share, width = qkv[0].shape
    rows = quarters * share
    padded = jax.ShapeDtypeStruct((rows + WIN, width), BF16)
    return pl.pallas_call(
        forward_kernel,
        out_shape=(
            jax.ShapeDtypeStruct((quarters, share, width), BF16),
            jax.ShapeDtypeStruct((rows, width), BF16),
            padded,
            padded,
        ),
        in_specs=vmem_specs(7),
        out_specs=(pl.BlockSpec(memory_space=pltpu.VMEM),) * 4,
        compiler_params=pltpu.CompilerParams(vmem_limit_bytes=40 * 2**20),
        cost_estimate=pl.CostEstimate(
            flops=16 * rows * WIN * width, bytes_accessed=16 * rows * width, transcendentals=0
        ),
        name="attend_forward",
    )(me, base, *qkv, *tables)


def attend_backward(me, base, queries, keys, values, grads, tables):
    quarters, share, width = grads.shape
    rows = quarters * share
    accumulator = pltpu.VMEM((rows + WIN, width), F32)
    return pl.pallas_call(
        backward_kernel,
        out_shape=jax.ShapeDtypeStruct((quarters, share, 3 * width), BF16),
        in_specs=vmem_specs(8),
        out_specs=pl.BlockSpec(memory_space=pltpu.VMEM),
        scratch_shapes=[accumulator, accumulator],
        compiler_params=pltpu.CompilerParams(vmem_limit_bytes=40 * 2**20),
        cost_estimate=pl.CostEstimate(
            flops=40 * rows * WIN * width, bytes_accessed=16 * rows * width, transcendentals=0
        ),
        name="attend_backward",
    )(me, base, queries, keys, values, grads, *tables)


def swap(tensor, bit):
    return lax.ppermute(tensor, "mp", [(i, i ^ bit) for i in range(4)])


def spread(rows):
    across = swap(rows, 2)
    return [rows, swap(rows, 1), across, swap(across, 1)]


def collect(product):
    away = [swap(product(r).astype(BF16), 1) for r in (3, 1)]
    across = swap((product(2) + away[0].astype(F32)).astype(BF16), 2)
    return product(0) + away[1].astype(F32) + across.astype(F32)


def dot_nt(left, right):
    return lax.dot_general(left, right, (((1,), (1,)), ((), ())), preferred_element_type=F32)


def dot_tn(left, right):
    return lax.dot_general(left, right, (((0,), (0,)), ((), ())), preferred_element_type=F32)


def bits_of(count):
    return [2**place for place in range(count.bit_length() - 1)]


def lowest(value):
    return value & -value


def greet(n, me, mp):
    barrier = pltpu.get_barrier_semaphore()
    partners = [{"dp": jnp.bitwise_xor(me, bit)} for bit in bits_of(n)]
    partners += [{"mp": jnp.bitwise_xor(mp, bit)} for bit in (1, 2)]
    for partner in partners:
        pl.semaphore_signal(barrier, inc=1, device_id=partner, device_id_type=MESH)
    pl.semaphore_wait(barrier, len(partners))


def remote(source, target, send_sem, recv_sem, axis, device):
    return pltpu.make_async_remote_copy(
        src_ref=source,
        dst_ref=target,
        send_sem=send_sem,
        recv_sem=recv_sem,
        device_id={axis: device},
        device_id_type=MESH,
    )


def gather_kernel(
    n, w_ref, g_ref, x_ref, s_ref, wo_ref, go_ref, xo_ref, so_ref, dp_send, dp_recv, mp_send, mp_recv
):
    me, mp = (lax.axis_index("dp"), lax.axis_index("mp"))
    greet(n, me, mp)
    pairs = ((w_ref, wo_ref), (g_ref, go_ref))
    bits = bits_of(n)[::-1]
    copies = []

    def forward(which, source, rel, owner):
        for bit in bits:
            if rel == 0 or bit < lowest(rel):
                copy = remote(
                    source,
                    pairs[which][1].at[owner],
                    dp_send.at[which, rel | bit],
                    dp_recv.at[which, rel | bit],
                    "dp",
                    jnp.bitwise_xor(me, bit),
                )
                copy.start()
                copies.append(copy)

    def arrive(rel):
        owner = jnp.bitwise_xor(me, rel)
        for which in (1, 0):
            block = pairs[which][1].at[owner]
            sems = (dp_send.at[which, rel], dp_recv.at[which, rel])
            remote(block, block, *sems, "dp", jnp.bitwise_xor(me, lowest(rel))).wait_recv()
            forward(which, block, rel, owner)

    def hand(which, source, slot, bit):
        copy = remote(
            source,
            (xo_ref, so_ref)[which].at[slot],
            mp_send.at[which, slot],
            mp_recv.at[which, slot],
            "mp",
            jnp.bitwise_xor(mp, bit),
        )
        copy.start()
        return copy

    for which in (1, 0):
        forward(which, pairs[which][0], 0, me)
    across = [hand(1, s_ref, 2, 2), hand(0, x_ref, 2, 2)]
    beside = [hand(1, s_ref, 1, 1), hand(0, x_ref, 1, 1)]
    wo_ref[me] = w_ref[...]
    go_ref[me] = g_ref[...]
    xo_ref[0] = x_ref[...]
    so_ref[0] = s_ref[...]
    order = sorted(range(1, n), key=lambda rel: (bin(rel).count("1"), -rel))
    for rel in order:
        if rel % 2 == 0:
            arrive(rel)
    corner = []
    for which, target in ((1, so_ref), (0, xo_ref)):
        across[1 - which].wait_recv()
        corner.append(hand(which, target.at[2], 3, 1))
    for rel in order:
        if rel % 2 == 1:
            arrive(rel)
    for copy in beside + corner:
        copy.wait_recv()
    for copy in copies + across + beside + corner:
        copy.wait_send()


def sum_kernel(
    n,
    q_ref,
    o_ref,
    g_ref,
    p_ref,
    rq_ref,
    ro_ref,
    rg_ref,
    rp_ref,
    q_in,
    o_in,
    g_in,
    q_out,
    o_out,
    g_out,
    p_in,
    p_out,
    g_mp,
    dp_send,
    dp_recv,
    p_send,
    p_recv,
    g_send,
    g_recv,
):
    me, mp = (lax.axis_index("dp"), lax.axis_index("mp"))
    greet(n, me, mp)
    sets = (
        (g_ref, g_in, g_out, rg_ref),
        (o_ref, o_in, o_out, ro_ref),
        (q_ref, q_in, q_out, rq_ref),
    )
    copies = []
    pieces = p_ref.shape[1] // WIN

    def launch(which, source, rel):
        copy = remote(
            source,
            sets[which][1].at[rel],
            dp_send.at[which, rel],
            dp_recv.at[which, rel],
            "dp",
            jnp.bitwise_xor(me, lowest(rel)),
        )
        copy.start()
        copies.append(copy)

    def total(which, rel):
        value = sets[which][0][jnp.bitwise_xor(me, rel)].astype(F32)
        arrivals = sets[which][1]
        for bit in bits_of(n):
            if rel == 0 or bit < lowest(rel):
                slot = rel | bit
                block = arrivals.at[slot]
                sems = (dp_send.at[which, slot], dp_recv.at[which, slot])
                remote(block, block, *sems, "dp", jnp.bitwise_xor(me, bit)).wait_recv()
                value = value + arrivals[slot].astype(F32)
        return value

    def hand(source, kind, piece, bit):
        copy = remote(
            source,
            p_in.at[kind, piece],
            p_send.at[kind, piece],
            p_recv.at[kind, piece],
            "mp",
            jnp.bitwise_xor(mp, bit),
        )
        copy.start()
        copies.append(copy)
        return copy

    levels = [
        [rel for rel in range(n - 1, 0, -1) if lowest(rel) == bit] for bit in bits_of(n)
    ]
    first = [rel | 1 for level in levels[1:] for rel in level] + [1]
    rows = [pl.ds(piece * WIN, WIN) for piece in range(pieces)]
    corner = [hand(p_ref.at[3, rows[i]], 0, i, 1) for i in range(pieces)]
    for rel in first:
        for which in range(3):
            launch(which, sets[which][0].at[jnp.bitwise_xor(me, rel)], rel)
    beside = [hand(p_ref.at[1, rows[i]], 1, i, 1) for i in range(pieces)]
    across = []
    for i in range(pieces):
        corner[i].wait_recv()
        p_out[i] = (p_ref[2, rows[i], :].astype(F32) + p_in[0, i].astype(F32)).astype(BF16)
        across.append(hand(p_out.at[i], 2, i, 2))
    for level in levels[1:]:
        for rel in level:
            for which in range(3):
                staged = sets[which][2]
                staged[rel] = total(which, rel).astype(staged.dtype)
                launch(which, staged.at[rel], rel)
    rg_ref[...] = total(0, 0)
    for step, bit in enumerate((1, 2)):
        g_mp[2 * step] = rg_ref[...]
        copy = remote(
            g_mp.at[2 * step],
            g_mp.at[2 * step + 1],
            g_send.at[step],
            g_recv.at[step],
            "mp",
            jnp.bitwise_xor(mp, bit),
        )
        copy.start()
        copies.append(copy)
        copy.wait_recv()
        rg_ref[...] = rg_ref[...] + g_mp[2 * step + 1]
    for i in range(pieces):
        beside[i].wait_recv()
        across[i].wait_recv()
        rp_ref[rows[i], :] = (
            p_ref[0, rows[i], :].astype(F32) + p_in[1, i].astype(F32) + p_in[2, i].astype(F32)
        )
    ro_ref[...] = total(1, 0)
    rq_ref[...] = total(2, 0)
    for copy in copies:
        copy.wait_send()


def comm_params(collective_id):
    return pltpu.CompilerParams(
        collective_id=collective_id, has_side_effects=True, vmem_limit_bytes=40 * 2**20
    )


def gather_all(weight, gain, rows, sequence):
    n = lax.axis_size("dp")
    vmem = pl.BlockSpec(memory_space=pltpu.VMEM)
    return pl.pallas_call(
        functools.partial(gather_kernel, n),
        out_shape=(
            jax.ShapeDtypeStruct((n,) + weight.shape, BF16),
            jax.ShapeDtypeStruct((n,) + gain.shape, F32),
            jax.ShapeDtypeStruct((4,) + rows.shape, BF16),
            jax.ShapeDtypeStruct((4,) + sequence.shape, jnp.int32),
        ),
        in_specs=[vmem] * 4,
        out_specs=(vmem,) * 4,
        scratch_shapes=[
            pltpu.SemaphoreType.DMA((2, n)),
            pltpu.SemaphoreType.DMA((2, n)),
            pltpu.SemaphoreType.DMA((2, 4)),
            pltpu.SemaphoreType.DMA((2, 4)),
        ],
        compiler_params=comm_params(0),
        name="gather_all",
    )(weight, gain, rows, sequence)


def sum_all(qkv, out, gain, products):
    n = lax.axis_size("dp")
    vmem = pl.BlockSpec(memory_space=pltpu.VMEM)
    pieces = products.shape[1] // WIN
    piece = (WIN, products.shape[2])
    return pl.pallas_call(
        functools.partial(sum_kernel, n),
        out_shape=tuple(
            jax.ShapeDtypeStruct(item.shape[1:], F32) for item in (qkv, out, gain, products)
        ),
        in_specs=[vmem] * 4,
        out_specs=(vmem,) * 4,
        scratch_shapes=[pltpu.VMEM(item.shape, item.dtype) for item in (qkv, out, gain)] * 2
        + [
            pltpu.VMEM((3, pieces) + piece, BF16),
            pltpu.VMEM((pieces,) + piece, BF16),
            pltpu.VMEM((4,) + gain.shape[1:], F32),
            pltpu.SemaphoreType.DMA((3, n)),
            pltpu.SemaphoreType.DMA((3, n)),
            pltpu.SemaphoreType.DMA((3, pieces)),
            pltpu.SemaphoreType.DMA((3, pieces)),
            pltpu.SemaphoreType.DMA((2,)),
            pltpu.SemaphoreType.DMA((2,)),
        ],
        compiler_params=comm_params(1),
        name="sum_all",
    )(qkv, out, gain, products)


def gather_columns(shard):
    parts = lax.all_gather(shard, "dp", axis=0)
    return jnp.transpose(parts, (1, 0, 2)).reshape(shard.shape[0], -1)


def scatter_rows(grad):
    return lax.psum_scatter(grad.astype(BF16), "dp", scatter_dimension=0, tiled=True).astype(F32)


def body(
    layer_input,
    row_seq,
    qkv_weight,
    out_weight,
    in_weight,
    down_weight,
    attn_gain,
    mlp_gain,
    cotangent,
):
    me = lax.axis_index("mp")
    me_arg = me.reshape(1).astype(jnp.int32)
    share, model = layer_input.shape
    width = qkv_weight.shape[2]
    units = in_weight.shape[2]
    own = attn_gain.shape[0]
    lanes = -(-own // 128) * 128
    gain_rows = jnp.pad(
        jnp.stack([attn_gain, mlp_gain]).astype(F32), ((0, 6), (0, lanes - own))
    )
    tiles = share // WIN
    first_shard = jnp.concatenate([qkv_weight.reshape(-1, 3 * width), out_weight.T], axis=1)
    first, gains, x_all, quarters = gather_all(
        first_shard,
        gain_rows,
        layer_input,
        jnp.pad(row_seq.reshape(tiles, WIN), ((0, -tiles % 8), (0, 0))),
    )
    first = first.reshape(model, 4 * width)
    w_qkv, w_out = (first[:, : 3 * width], first[:, 3 * width :])
    gain_one, gain_two = (gains[:, row, :own].reshape(model) for row in range(2))
    w_gate, w_up, w_down = [
        lax.all_gather(item, "dp", axis=0, tiled=True)
        for item in (in_weight[:, 0], in_weight[:, 1], down_weight.T)
    ]

    seq_all = jnp.take(quarters[:, :tiles], jnp.arange(4) ^ me, axis=0).reshape(-1)
    group_rows = seq_all.shape[0]
    blocks = group_rows // WIN
    base = positions(seq_all.reshape(blocks, WIN)[:, 0])
    padded_seq = jnp.pad(seq_all, (WIN // 2, WIN // 2), constant_values=-5).reshape(-1, WIN)
    seq_rows = jnp.concatenate([padded_seq[:-1], padded_seq[1:]], axis=1).reshape(
        blocks, 1, 2 * WIN
    )
    tables = (*rotation_tables(group_rows), seq_all[:, None], seq_rows)

    grad_final = cotangent.astype(F32) * (row_seq >= 0).astype(F32)[:, None]
    grad_parts = spread(grad_final.astype(BF16))

    block_in = layer_input.astype(F32)
    normed_one, factor_one = normalize(block_in)
    normed_all = normalize(x_all.reshape(-1, model).astype(F32))[0]
    h_all = (normed_all * gain_one).astype(BF16)
    qkv = [
        jnp.dot(
            h_all, w_qkv[:, part * width : (part + 1) * width], preferred_element_type=F32
        ).reshape(4, share, width)
        for part in range(3)
    ]
    mixed, queries, keys, values = attend_forward(me_arg, base, qkv, tables)
    grad_parts, mixed = lax.optimization_barrier((grad_parts, mixed))
    middle = block_in + collect(
        lambda r: dot_nt(mixed[r], w_out)
    )
    normed_two, factor_two = normalize(middle)
    h2_own = (normed_two * gain_two).astype(BF16)
    h2_across = swap(h2_own, 2)
    h2_parts = [h2_own, swap(h2_own, 1)]

    def product(gate_in, up_in):
        return jax.nn.gelu(gate_in, approximate=False) * up_in

    halves = []
    for start in (0, 2):
        if start:
            h2_across, ready = lax.optimization_barrier((h2_across, halves[0][2]))
            halves[0] = halves[0][:2] + (ready,) + halves[0][3:]
            h2_parts += [h2_across, swap(h2_across, 1)]
        h_rows = jnp.concatenate(h2_parts[start : start + 2], axis=0)
        g_rows = jnp.concatenate(grad_parts[start : start + 2], axis=0)
        gate_vals = jnp.dot(h_rows, w_gate, preferred_element_type=F32)
        up_values = jnp.dot(h_rows, w_up, preferred_element_type=F32)
        value, pullback = jax.vjp(product, gate_vals, up_values)
        grad_gate, grad_up = pullback(jnp.dot(g_rows, w_down, preferred_element_type=F32))
        halves.append(
            (h_rows, g_rows, value.astype(BF16), grad_gate.astype(BF16), grad_up.astype(BF16))
        )

    def quarter_of(part, r):
        return halves[r // 2][part][(r % 2) * share : (r % 2 + 1) * share]

    grad_h_two = collect(
        lambda r: dot_nt(quarter_of(3, r), w_gate) + dot_nt(quarter_of(4, r), w_up)
    )
    h2_all, grad_all, hidden, grad_gate, grad_up = [
        jnp.concatenate(pair, axis=0) for pair in zip(*halves)
    ]
    down_share = scatter_rows(dot_tn(grad_all, hidden)).T
    in_partial = jnp.concatenate(
        [dot_tn(h2_all, grad_gate).astype(BF16), dot_tn(h2_all, grad_up).astype(BF16)], axis=1
    )
    grad_norm_two, gain_two_grad = norm_back(grad_h_two, normed_two, factor_two, gain_two)
    grad_middle = grad_final + grad_norm_two
    grad_mid_own, in_partial, late_hidden = lax.optimization_barrier(
        (grad_middle.astype(BF16), in_partial, [item[2] for item in halves])
    )
    in_share = scatter_rows(in_partial).reshape(-1, 2, units)
    grad_mid_all = jnp.concatenate(spread(grad_mid_own), axis=0)
    activations = (
        middle
        + collect(
            lambda r: dot_nt(
                late_hidden[r // 2][(r % 2) * share : (r % 2 + 1) * share], w_down
            )
        )
    ).astype(BF16)
    grad_mixed = jnp.dot(grad_mid_all, w_out, preferred_element_type=F32).astype(BF16).reshape(4, share, width)
    grad_qkv = attend_backward(me_arg, base, queries, keys, values, grad_mixed, tables)
    flat_grad = grad_qkv.reshape(group_rows, 3 * width)
    n = lax.axis_size("dp")
    products = dot_nt(flat_grad, w_qkv)
    gain_one_grad = jnp.sum(products * normed_all, axis=0)
    gain_grads = jnp.stack([gain_one_grad, gain_two_grad]).reshape(2, n, own)
    gain_grads = jnp.pad(jnp.transpose(gain_grads, (1, 0, 2)), ((0, 0), (0, 6), (0, lanes - own)))
    qkv_share, out_share, gain_total, grad_h_one = sum_all(
        dot_tn(h_all, flat_grad).astype(BF16).reshape(n, -1, 3 * width),
        dot_tn(grad_mid_all, mixed.reshape(group_rows, width)).astype(BF16).reshape(n, -1, width),
        gain_grads,
        products.astype(BF16).reshape(4, share, model),
    )
    grad_norm_one, _ = norm_back(grad_h_one, normed_one, factor_one, gain_one)
    input_grad = (grad_middle + grad_norm_one).astype(BF16)
    qkv_share = qkv_share.reshape(-1, 3, width)
    out_share = out_share.T
    gain_total = gain_total[:2, :own]
    return (
        activations,
        input_grad,
        gain_total[0],
        gain_total[1],
        qkv_share,
        out_share,
        in_share,
        down_share,
    )


def solution(mesh):
    in_specs = (
        P(("dp", "mp"), None),
        P(("dp", "mp")),
        P("dp", None, "mp"),
        P("mp", "dp"),
        P("dp", None, "mp"),
        P("mp", "dp"),
        P("dp"),
        P("dp"),
        P(("dp", "mp"), None),
    )
    out_specs = (
        P(("dp", "mp"), None),
        P(("dp", "mp"), None),
        P("dp"),
        P("dp"),
        P("dp", None, "mp"),
        P("mp", "dp"),
        P("dp", None, "mp"),
        P("mp", "dp"),
    )
    return jax.shard_map(body, mesh=mesh, in_specs=in_specs, out_specs=out_specs, check_vma=False)
```
